128 devices in a mesh: tm: 8 (over x, core), mem: 16 (over y, z).
Axes of the slice: x: 4, y: 4, z: 4, core: 2. Of those that a mesh axis runs over, the one named last changes fastest.
Arguments:
- tokens: bfloat16 [32768, 2048], P(('tm', 'mem')), may hold values from -6 to 6
- queries: bfloat16 [32768, 2048], P(('tm', 'mem')), may hold values from -6 to 6
- log_decay: bfloat16 [32768, 16], P(('tm', 'mem')), may hold values from -1 to 0
- route_ids: int32 [32768, 2], P(('tm', 'mem')), may hold values from 0 to 15, all different within a row; in each aligned block of 256 rows (0 to 255, 256 to 511, ...) at most 48 rows name the same one
- gate_weights: float32 [32768, 2], P(('tm', 'mem')), may hold values from 0.3 to 1
- kv_weight: bfloat16 [16, 2048, 4096], P('mem'), may hold values from -0.125 to 0.125
Outputs:
- mixed: bfloat16 [32768, 2048], P(('tm', 'mem'))
The draws below stay inside these ranges and needn't reach their ends.
Inputs may be any that keep to these rules, and one draw needn't show every extreme that they name: `route_ids`: each row names 2 different memories. In each aligned block of 256 rows (the rows of one device) no memory is named by more than 48 rows, and in some block one memory is named by exactly 48 rows.
All inputs are finite; a program needn't handle non-finite values.
Results may differ from the reference program's by a relative error of at most 0.006.
Values may be sent and summed in bfloat16 or wider, within the bound.
A program may use at most 128 MiB of HBM per device.

```python
import math
import jax
import jax.numpy as jnp
import numpy as np
from jax import lax

D = 2048
H = 16
HD = 128
TOP = 2
TOK_DEV = 256
STATE_COUNT = 16
WORD_COUNT = 32768
CAP = 48
N_TM = 8
N_MEM = 16


def draw_log_decay(key, part):
    derived_seed_list = jax.random.split(key, 7)
    chain_mean = WORD_COUNT * TOP / STATE_COUNT
    slow_heads = jax.random.uniform(derived_seed_list[0], (H,)) < 0.5
    fast_rate = jnp.exp(jax.random.uniform(derived_seed_list[1], (H,), minval=math.log(1.0 / 50.0), maxval=math.log(1.0 / 30.0)))
    slow_rate = jnp.exp(jax.random.uniform(derived_seed_list[2], (H,), minval=math.log(0.2), maxval=0.0)) / chain_mean
    rates = jnp.where(slow_heads, slow_rate, fast_rate)
    rough = jnp.exp(jax.random.uniform(derived_seed_list[3], (WORD_COUNT, H), minval=-math.log(2.0), maxval=math.log(2.0)))
    device_factor = jnp.exp(jax.random.uniform(derived_seed_list[4], (WORD_COUNT // TOK_DEV, 1, H), minval=-math.log(2.0), maxval=math.log(2.0)))
    starting_shift = -(rates[None, :] * rough).reshape(WORD_COUNT // TOK_DEV, TOK_DEV, H) * device_factor
    starting_shift = starting_shift.reshape(WORD_COUNT, H)
    span_extent = jax.random.randint(derived_seed_list[5], (WORD_COUNT, 1), 0, WORD_COUNT) < max(STATE_COUNT // 2, 1)
    stack_level = jax.random.uniform(derived_seed_list[6], (WORD_COUNT, H), minval=math.log(0.5), maxval=math.log(0.8))
    emitted_result = starting_shift + jnp.where(span_extent, stack_level, 0.0)
    return emitted_result.astype(jnp.float32).astype(jnp.bfloat16)


def level_of(own_key, extent, cuts, smallest, top_value):
    gain, own = 1.0, jax.random.fold_in(own_key, 6)
    for dim, blocks in cuts:
        heights = jnp.exp(jax.random.uniform(jax.random.fold_in(own, dim), (blocks,), jnp.float32, smallest / len(cuts), top_value / len(cuts)))
        gain = gain * jnp.repeat(heights, extent[dim] // blocks).reshape([-1 if axis == dim else 1 for axis in range(len(extent))])
    return gain


def routed_block(rng, own, number, rows, amount, top, limit, slope):
    ranking = jax.random.permutation(rng, amount)
    crowded, common = load_shares(amount, rows * top, limit, slope, True), load_shares(amount, rows * top, limit, slope, False)
    places = jnp.arange(amount)

    def named(lengths, turn):
        used = int((lengths > 0).sum())
        fixed = max(1, used // 4)
        moved = fixed + (places - fixed + turn * (used - fixed)) % max(1, amount - fixed)
        return jnp.zeros((amount,), jnp.int32).at[ranking[jnp.where(places < fixed, places, moved)]].set(jnp.asarray(lengths, jnp.int32))

    lengths = jnp.where(number % 4 == 0, named(crowded, number // 4), named(common, number - number // 4 - 1))
    mixed = jax.random.permutation(jax.random.fold_in(own, 3), amount)
    giver, taker = mixed[0:amount // 2 * 2:2], mixed[1:amount // 2 * 2:2]
    margin = jnp.minimum(lengths[giver] - 1, limit - lengths[taker]) // 2
    margin = jnp.where((giver == ranking[0]) | (taker == ranking[0]) | (lengths[taker] == 0), 0, jnp.maximum(margin, 0))
    moved = jax.random.randint(jax.random.fold_in(own, 4), (amount // 2,), 0, 1 << 20) % (margin + 1)
    lengths = lengths.at[giver].add(-moved).at[taker].add(moved)
    labels = jnp.searchsorted(jnp.cumsum(lengths), jnp.arange(rows * top), side="right").astype(jnp.int32)
    grid = labels.reshape(top, rows).T
    grid = grid[jax.random.permutation(jax.random.fold_in(own, 1), rows)]
    turn = jax.random.randint(jax.random.fold_in(own, 2), (rows, 1), 0, top)
    return jnp.take_along_axis(grid, (jnp.arange(top)[None, :] + turn) % top, axis=1)


def load_shares(number_of, total, limit, skew, full):
    portions = [(1 << 20) // math.isqrt(rank ** skew) + 1 for rank in range(1, number_of + 1)]
    largest = limit if full else min(limit, max(-(-total // number_of), total * portions[0] // sum(portions)))
    least = 1 if total - largest >= number_of - 1 else 0
    counts, spare = [largest] + [least] * (number_of - 1), total - largest - least * (number_of - 1)
    while spare > 0:
        candidates = [i for i in range(1, number_of) if counts[i] < largest] or [i for i in range(1, number_of) if counts[i] < limit]
        whole, budget = sum([portions[i] for i in candidates]), spare
        for i in candidates:
            more = min(limit - counts[i], max(1, budget * portions[i] // whole), spare)
            counts[i] = counts[i] + more
            spare = spare - more
    return np.array(counts)


def centred(key, shape, scale, bound, cuts=(), kind=jnp.bfloat16):
    array = jax.random.normal(key, shape, jnp.float32) * scale
    if len(cuts) > 0:
        array = level_of(key, shape, cuts, -0.22, 0.18) * array
    return jnp.clip(array, min=-bound, max=bound).astype(kind)


def setup_inputs(seed: int = 0) -> dict:
    splits = jax.random.split(jax.random.key(seed), 7)
    tokens = centred(splits[0], (WORD_COUNT, D), 1.0, 6.0, ((0, 128),))
    queries = centred(splits[1], (WORD_COUNT, D), 1.0, 6.0, ((0, 128),))
    log_decay = draw_log_decay(jax.random.fold_in(splits[6], 71), 0)
    route_ids_keys = jax.random.split(jax.random.fold_in(splits[3], 1), WORD_COUNT // TOK_DEV)
    route_ids_turns = jax.random.permutation(jax.random.fold_in(splits[3], 3), WORD_COUNT // TOK_DEV)
    route_ids = jax.vmap(lambda own, number: routed_block(jax.random.fold_in(splits[3], 2), own, number, TOK_DEV, STATE_COUNT, TOP, CAP, 2))(route_ids_keys, route_ids_turns).reshape((WORD_COUNT, TOP))
    gate_weights = jnp.clip(0.3 + 0.7 * jax.random.uniform(splits[4], (WORD_COUNT, TOP), jnp.float32) ** level_of(splits[4], (WORD_COUNT, TOP), ((0, 128),), -0.2, 0.2), 0.3, 1.0)
    kv_weight = centred(splits[5], (STATE_COUNT, D, 2 * D), D ** -0.5, 0.125, ((0, 16),))
    return dict(tokens=tokens, queries=queries, log_decay=log_decay, route_ids=route_ids, gate_weights=gate_weights, kv_weight=kv_weight)


exact_mode = lax.Precision.HIGHEST

def block_pass(queries_heads, keys_heads, values_heads, decay_logs, block_rows):
    head_count, chain_rows, head_size = queries_heads.shape
    block_count = chain_rows // block_rows

    def split_blocks(tensor):
        return jnp.moveaxis(tensor.reshape(head_count, block_count, block_rows, head_size), 1, 0)
    blocked = (split_blocks(queries_heads), split_blocks(keys_heads), split_blocks(values_heads), jnp.moveaxis(decay_logs.reshape(head_count, block_count, block_rows), 1, 0))
    lower = jnp.arange(block_rows)[:, None] >= jnp.arange(block_rows)[None, :]

    def advance(carried, pieces):
        query_block, key_block, value_block, log_block = pieces
        running = jnp.cumsum(log_block, axis=1)
        spread = jnp.minimum(running[:, :, None] - running[:, None, :], 0.0)
        weights = jnp.where(lower[None], jnp.exp(spread), 0.0)
        scores = jnp.einsum('hnd,hid->hni', query_block, key_block, preferred_element_type=jnp.float32) * weights
        value_wide = value_block.astype(jnp.float32)
        within = jnp.einsum('hni,hie->hne', scores, value_wide, precision=exact_mode)
        earlier = jnp.einsum('hnd,hde->hne', query_block.astype(jnp.float32), carried, precision=exact_mode) * jnp.exp(running)[:, :, None]
        ending = running[:, -1]
        fading = jnp.exp(ending[:, None] - running)
        carried = jnp.exp(ending)[:, None, None] * carried + jnp.einsum('hid,hie->hde', key_block.astype(jnp.float32) * fading[:, :, None], value_wide, precision=exact_mode)
        return (carried, within + earlier)
    start = jnp.zeros((head_count, head_size, head_size), jnp.float32)
    final_state, outputs = lax.scan(advance, start, blocked)
    outputs = jnp.moveaxis(outputs, 0, 1).reshape(head_count, chain_rows, head_size)
    return (final_state, outputs)

def normalize(outputs):
    mean_square = lax.optimization_barrier(jnp.mean(outputs * outputs, axis=-1, keepdims=True))
    return outputs * lax.rsqrt(mean_square + 1e-06)

def reference(tokens, queries, log_decay, route_ids, gate_weights, kv_weight):
    chain_len = N_TM * N_MEM * CAP
    block_rows = math.gcd(chain_len, 512)
    positions = jnp.arange(WORD_COUNT, dtype=jnp.int32)

    def one_memory(total, memory):
        named = route_ids == memory
        routed = jnp.any(named, axis=1)
        order_key = jnp.where(routed, positions, WORD_COUNT + positions).astype(jnp.int32)
        picked = jnp.argsort(order_key)[:chain_len].astype(jnp.int32)
        valid = routed[picked]
        chain_x = jnp.where(valid[:, None], tokens[picked], jnp.zeros((), jnp.bfloat16))
        weight_now = lax.dynamic_index_in_dim(kv_weight, memory, 0, keepdims=False)
        projected = jnp.dot(chain_x, weight_now, preferred_element_type=jnp.float32).astype(jnp.bfloat16)
        keys_heads = projected[:, :D].reshape(chain_len, H, HD).transpose(1, 0, 2)
        values_heads = projected[:, D:].reshape(chain_len, H, HD).transpose(1, 0, 2)
        query_heads = queries[picked].reshape(chain_len, H, HD).transpose(1, 0, 2)
        logs_heads = jnp.where(valid[:, None], log_decay[picked].astype(jnp.float32), 0.0).T
        final_state, outputs = block_pass(query_heads, keys_heads, values_heads, logs_heads, block_rows)
        normed = normalize(outputs).astype(jnp.bfloat16).transpose(1, 0, 2).reshape(chain_len, D)
        gate_here = lax.optimization_barrier(jnp.sum(jnp.where(named, gate_weights, 0.0), axis=1))[picked]
        gate_here = jnp.where(valid, gate_here, 0.0)
        total = total.at[picked].add(gate_here[:, None] * normed.astype(jnp.float32))
        return (total, None)
    start = jnp.zeros((WORD_COUNT, D), jnp.float32)
    total, unused = lax.scan(one_memory, start, jnp.arange(STATE_COUNT, dtype=jnp.int32))
    return total.astype(jnp.bfloat16)
```

```python
import functools

import jax
import jax.numpy as jnp
from jax import lax
from jax.experimental import pallas as pl
from jax.experimental.pallas import tpu as pltpu
from jax.sharding import PartitionSpec as P

MESH = pl.DeviceIdType.MESH
F32, BF16 = jnp.float32, jnp.bfloat16

MEM_Y, MEM_Z = 4, 4
MEMBERS = MEM_Y * MEM_Z
TM = 8
TOK = 256
CAP = 48
ROWS = MEMBERS * CAP
D = 2048
H = 16
HD = 128
XW = D + 128
CHUNK = 256
CHUNKS = ROWS // CHUNK
GROUPS = 4
GW = D // GROUPS
GH = H // GROUPS
PAIRS = H // 2
GP = PAIRS // GROUPS

SHIFTS = (
    (1, 0), (3, 0), (0, 1), (0, 3),
    (1, 1), (3, 3), (1, 3), (3, 1),
    (2, 1), (2, 3), (1, 2), (3, 2),
    (2, 0), (0, 2), (2, 2),
)
PEERS = len(SHIFTS)
BACK = 3


def mm(a, b, da=1, db=0):
    return lax.dot_general(a, b, (((da,), (db,)), ((), ())), preferred_element_type=F32)


def kernel(
    tok_hbm, qry_hbm, dec_ref, route_ref, gate_ref, w_hbm, out_hbm,
    tok, qry, w, onehot, chi, clo,
    sendx, recvx, sendq, recvq, kb, vb, osend, ret, outb,
    rcol, rrow, ends, atot, aprev, ub, inc, exc, ssend, srecv,
    load_sem, xs, xr, qs, qr, os_, or_, as_, ar, ss, sr, out_sem,
):
    tm = lax.axis_index("tm")
    me = lax.axis_index("mem")
    my, mz = lax.div(me, MEM_Z), lax.rem(me, MEM_Z)

    def at(dy, dz):
        return lax.rem(my + dy, MEM_Y) * MEM_Z + lax.rem(mz + dz, MEM_Z)

    to = [at(dy, dz) for dy, dz in SHIFTS]
    source = [at(MEM_Y - dy, MEM_Z - dz) for dy, dz in SHIFTS]

    def block(place):
        return pl.ds(pl.multiple_of(place * CAP, 16), CAP)

    barrier = pltpu.get_barrier_semaphore()
    for i in range(PEERS):
        pl.semaphore_signal(barrier, inc=1, device_id=(tm, to[i]), device_id_type=MESH)
    for d in range(1, TM):
        pl.semaphore_signal(
            barrier, inc=1, device_id=(lax.rem(tm + d, TM), me), device_id_type=MESH
        )

    load_tok = pltpu.make_async_copy(tok_hbm, tok, load_sem.at[0])
    load_qry = pltpu.make_async_copy(qry_hbm, qry, load_sem.at[1])
    load_w = pltpu.make_async_copy(w_hbm.at[0], w, load_sem.at[2])
    load_tok.start()
    load_qry.start()
    load_w.start()

    r0, r1 = route_ref[0:1, :], route_ref[1:2, :]
    mem_row = lax.broadcasted_iota(jnp.int32, (MEMBERS, TOK), 0)
    hot0 = (mem_row == r0).astype(F32)
    hot1 = (mem_row == r1).astype(F32)
    ahead = (
        lax.broadcasted_iota(jnp.int32, (TOK, TOK), 0)
        < lax.broadcasted_iota(jnp.int32, (TOK, TOK), 1)
    ).astype(BF16)
    rank = mm((hot0 + hot1).astype(BF16), ahead)
    slot0 = r0 * CAP + jnp.sum(hot0 * rank, axis=0, keepdims=True).astype(jnp.int32)
    slot1 = r1 * CAP + jnp.sum(hot1 * rank, axis=0, keepdims=True).astype(jnp.int32)
    slot_row = lax.broadcasted_iota(jnp.int32, (ROWS, TOK), 0)
    is0, is1 = slot_row == slot0, slot_row == slot1
    onehot[...] = (is0.astype(F32) + is1.astype(F32)).astype(BF16)

    for r in range(3):

        @pl.when(tm < (1 << r))
        def _():
            srecv[r] = jnp.zeros((H, HD, HD), BF16)

    for d in range(1, BACK + 1):

        @pl.when(tm < d)
        def _():
            aprev[d - 1] = jnp.zeros((H, HD), F32)

    dec_wide = jnp.concatenate([dec_ref[...], jnp.zeros((128 - H, TOK), BF16)], axis=0)
    sendx[:, D:XW] = mm(onehot[...], dec_wide, 1, 1).astype(BF16)
    load_tok.wait()

    def gather_x(j, c):
        cols = pl.ds(pl.multiple_of(j * 256, 256), 256)
        sendx[:, cols] = mm(onehot[...], tok[:, cols]).astype(BF16)
        return c

    lax.fori_loop(0, D // 256, gather_x, 0)
    pl.semaphore_wait(barrier, PEERS + TM - 1)

    def x_copy(i, src, dst):
        return pltpu.make_async_remote_copy(
            src_ref=sendx.at[block(src)],
            dst_ref=recvx.at[block(dst)],
            send_sem=xs.at[i],
            recv_sem=xr.at[i],
            device_id=(tm, to[i]),
            device_id_type=MESH,
        )

    def q_copy(g, i, src, dst):
        return pltpu.make_async_remote_copy(
            src_ref=sendq.at[g, block(src)],
            dst_ref=recvq.at[g, block(dst)],
            send_sem=qs.at[g, i],
            recv_sem=qr.at[g, i],
            device_id=(tm, to[i]),
            device_id_type=MESH,
        )

    def o_copy(g, i, src, dst):
        return pltpu.make_async_remote_copy(
            src_ref=osend.at[g, block(src)],
            dst_ref=ret.at[g, block(dst)],
            send_sem=os_.at[g, i],
            recv_sem=or_.at[g, i],
            device_id=(tm, to[i]),
            device_id_type=MESH,
        )

    def a_copy(d):
        return pltpu.make_async_remote_copy(
            src_ref=atot,
            dst_ref=aprev.at[d - 1],
            send_sem=as_.at[d - 1],
            recv_sem=ar.at[d - 1],
            device_id=(lax.rem(tm + d, TM), me),
            device_id_type=MESH,
        )

    def s_copy(r, g):
        heads = pl.ds(g * GH, GH)
        return pltpu.make_async_remote_copy(
            src_ref=ssend.at[r, heads],
            dst_ref=srecv.at[r, heads],
            send_sem=ss.at[r, g],
            recv_sem=sr.at[r, g],
            device_id=(lax.rem(tm + (1 << r), TM), me),
            device_id_type=MESH,
        )

    for i in range(PEERS):
        x_copy(i, to[i], me).start()

    load_qry.wait()

    def gather_q(g, c):
        for half in range(GW // 256):
            cols = pl.ds(pl.multiple_of(g * GW + half * 256, 256), 256)
            sendq[g, :, half * 256 : half * 256 + 256] = mm(onehot[...], qry[:, cols]).astype(BF16)
        for i in range(PEERS):
            q_copy(g, i, to[i], me).start()
        recvq[g, block(me), :] = sendq[g, block(me), :]
        return c

    lax.fori_loop(0, GROUPS, gather_q, 0)
    recvx[block(me), :] = sendx[block(me), :]

    gates = jnp.where(is0, gate_ref[0:1, :], 0.0) + jnp.where(is1, gate_ref[1:2, :], 0.0)
    gates_hi = gates.astype(BF16)
    chi[...] = gates_hi.T
    clo[...] = (gates - gates_hi.astype(F32)).astype(BF16).T

    load_w.wait()
    for i in range(PEERS):
        x_copy(i, to[i], source[i]).wait_recv()

    tri_r = lax.broadcasted_iota(jnp.int32, (CHUNK, CHUNK), 0)
    tri_c = lax.broadcasted_iota(jnp.int32, (CHUNK, CHUNK), 1)
    lower = (tri_r >= tri_c).astype(BF16)
    total = jnp.zeros((H, HD), F32)
    for c in range(CHUNKS):
        logs = recvx[c * CHUNK : (c + 1) * CHUNK, D:XW]
        rcol[c] = mm(lower, logs)
        rows = mm(logs, lower, 0, 1)[:H]
        rrow[c] = rows
        end = jnp.broadcast_to(rows[:, CHUNK - 1 : CHUNK], (H, HD))
        ends[c] = end
        total = total + end
    atot[...] = total
    for d in range(1, BACK + 1):

        @pl.when(tm + d < TM)
        def _():
            a_copy(d).start()

    lane = lax.broadcasted_iota(jnp.int32, (CHUNK, HD), 1)

    def column(c, h):
        return jnp.sum(jnp.where(lane == h, rcol[c], 0.0), axis=1, keepdims=True)

    def project(j, carry):
        kcols = pl.ds(pl.multiple_of(j * 256, 256), 256)
        vcols = pl.ds(pl.multiple_of(D + j * 256, 256), 256)
        kb[j] = mm(recvx[:, :D], w[:, kcols]).astype(BF16)
        vb[j] = mm(recvx[:, :D], w[:, vcols]).astype(BF16)
        for hh in range(2):
            h = 2 * j + hh
            lanes = slice(hh * HD, hh * HD + HD)
            local = None
            for c in range(CHUNKS):
                rows = slice(c * CHUNK, (c + 1) * CHUNK)
                end = ends[c, pl.ds(h, 1), :]
                fade = jnp.exp(end - column(c, h))
                keys = (kb[j, rows, lanes].astype(F32) * fade).astype(BF16)
                part = mm(keys, vb[j, rows, lanes], 0, 0)
                if c < CHUNKS - 1:
                    ub[c, h] = part
                local = part if c == 0 else jnp.exp(end) * local + part
            inc[h] = local
            ssend[0, h] = local.astype(BF16)
        return carry

    def gain(h, first, last):
        span = aprev[first, pl.ds(h, 1), :]
        for d in range(first + 1, last):
            span = span + aprev[d, pl.ds(h, 1), :]
        return span

    def round0(h, carry):
        got = srecv[0, h].astype(F32)
        exc[h] = got
        new = jnp.exp(atot[pl.ds(h, 1), :]) * got + inc[h]
        inc[h] = new
        ssend[1, h] = new.astype(BF16)
        return carry

    def round1(h, carry):
        got = srecv[1, h].astype(F32)
        before = gain(h, 0, 1)
        exc[h] = jnp.exp(before) * got + exc[h]
        new = jnp.exp(before + atot[pl.ds(h, 1), :]) * got + inc[h]
        ssend[2, h] = new.astype(BF16)
        return carry

    def round2(h, carry):
        got = srecv[2, h].astype(F32)
        exc[h] = jnp.exp(gain(h, 0, 3)) * got + exc[h]
        return carry

    def send_state(r, g):
        @pl.when(tm + (1 << r) < TM)
        def _():
            s_copy(r, g).start()

    def take_state(r, g):
        @pl.when(tm >= (1 << r))
        def _():
            s_copy(r, g).wait_recv()

    def stage(s, carry):
        @pl.when(s < GROUPS)
        def _():
            lax.fori_loop(s * GP, (s + 1) * GP, project, 0)
            send_state(0, s)

        @pl.when(s == 0)
        def _():
            for d in range(1, BACK + 1):

                @pl.when(tm >= d)
                def _():
                    a_copy(d).wait_recv()

        for r, step in enumerate((round0, round1, round2)):
            g = s - 1 - r

            @pl.when(jnp.logical_and(g >= 0, g < GROUPS))
            def _():
                take_state(r, g)
                lax.fori_loop(g * GH, (g + 1) * GH, step, 0)
                if r < 2:
                    send_state(r + 1, g)

        return carry

    lax.fori_loop(0, GROUPS + 3, stage, 0)

    def emit(g, carry):
        for i in range(PEERS):
            q_copy(g, i, to[i], source[i]).wait_recv()

        def head(hh, inner):
            h = g * GH + hh
            j = lax.div(h, 2)
            klanes = pl.ds(pl.multiple_of(lax.rem(h, 2) * HD, HD), HD)
            qlanes = pl.ds(pl.multiple_of(hh * HD, HD), HD)
            state = exc[h]
            for c in range(CHUNKS):
                rows = slice(c * CHUNK, (c + 1) * CHUNK)
                q = recvq[g, rows, qlanes]
                k = kb[j, rows, klanes]
                v = vb[j, rows, klanes]
                col = column(c, h)
                spread = jnp.exp(jnp.minimum(col - rrow[c, pl.ds(h, 1), :], 0.0))
                scores = jnp.where(tri_r >= tri_c, mm(q, k, 1, 1) * spread, 0.0)
                o = mm(scores.astype(BF16), v) + mm(q, state.astype(BF16)) * jnp.exp(col)
                scale = lax.rsqrt(jnp.mean(o * o, axis=1, keepdims=True) + 1e-06)
                osend[g, rows, qlanes] = (o * scale).astype(BF16)
                if c < CHUNKS - 1:
                    state = jnp.exp(ends[c, pl.ds(h, 1), :]) * state + ub[c, h]
            return inner

        lax.fori_loop(0, GH, head, 0)
        for i in range(PEERS):
            o_copy(g, i, to[i], me).start()
        ret[g, block(me), :] = osend[g, block(me), :]
        return carry

    lax.fori_loop(0, GROUPS, emit, 0)

    def out_copy(g):
        cols = pl.ds(pl.multiple_of(g * GW, GW), GW)
        return pltpu.make_async_copy(outb.at[:, cols], out_hbm.at[:, cols], out_sem.at[g])

    def finish(g, carry):
        for i in range(PEERS):
            o_copy(g, i, to[i], source[i]).wait_recv()
        for half in range(GW // 256):
            cols = slice(half * 256, half * 256 + 256)
            where = pl.ds(pl.multiple_of(g * GW + half * 256, 256), 256)
            got = ret[g, :, cols]
            outb[:, where] = (mm(chi[...], got) + mm(clo[...], got)).astype(BF16)
        out_copy(g).start()
        return carry

    lax.fori_loop(0, GROUPS, finish, 0)

    for i in range(PEERS):
        x_copy(i, to[i], me).wait_send()

    def sent(g, carry):
        for i in range(PEERS):
            q_copy(g, i, to[i], me).wait_send()
            o_copy(g, i, to[i], me).wait_send()
        for r in range(3):

            @pl.when(tm + (1 << r) < TM)
            def _():
                s_copy(r, g).wait_send()

        out_copy(g).wait()
        return carry

    lax.fori_loop(0, GROUPS, sent, 0)
    for d in range(1, BACK + 1):

        @pl.when(tm + d < TM)
        def _():
            a_copy(d).wait_send()


def on_device(tokens, queries, log_decay, route_ids, gate_weights, kv_weight):
    anywhere = pl.BlockSpec(memory_space=pl.ANY)
    near = pl.BlockSpec(memory_space=pltpu.VMEM)
    dma = pltpu.SemaphoreType.DMA
    return pl.pallas_call(
        kernel,
        out_shape=jax.ShapeDtypeStruct((TOK, D), BF16),
        in_specs=[anywhere, anywhere, near, near, near, anywhere],
        out_specs=anywhere,
        scratch_shapes=[
            pltpu.VMEM((TOK, D), BF16),
            pltpu.VMEM((TOK, D), BF16),
            pltpu.VMEM((D, 2 * D), BF16),
            pltpu.VMEM((ROWS, TOK), BF16),
            pltpu.VMEM((TOK, ROWS), BF16),
            pltpu.VMEM((TOK, ROWS), BF16),
            pltpu.VMEM((ROWS, XW), BF16),
            pltpu.VMEM((ROWS, XW), BF16),
            pltpu.VMEM((GROUPS, ROWS, GW), BF16),
            pltpu.VMEM((GROUPS, ROWS, GW), BF16),
            pltpu.VMEM((PAIRS, ROWS, 256), BF16),
            pltpu.VMEM((PAIRS, ROWS, 256), BF16),
            pltpu.VMEM((GROUPS, ROWS, GW), BF16),
            pltpu.VMEM((GROUPS, ROWS, GW), BF16),
            pltpu.VMEM((TOK, D), BF16),
            pltpu.VMEM((CHUNKS, CHUNK, HD), F32),
            pltpu.VMEM((CHUNKS, H, CHUNK), F32),
            pltpu.VMEM((CHUNKS, H, HD), F32),
            pltpu.VMEM((H, HD), F32),
            pltpu.VMEM((BACK, H, HD), F32),
            pltpu.VMEM((CHUNKS - 1, H, HD, HD), F32),
            pltpu.VMEM((H, HD, HD), F32),
            pltpu.VMEM((H, HD, HD), F32),
            pltpu.VMEM((3, H, HD, HD), BF16),
            pltpu.VMEM((3, H, HD, HD), BF16),
            dma((3,)),
            dma((PEERS,)),
            dma((PEERS,)),
            dma((GROUPS, PEERS)),
            dma((GROUPS, PEERS)),
            dma((GROUPS, PEERS)),
            dma((GROUPS, PEERS)),
            dma((BACK,)),
            dma((BACK,)),
            dma((3, GROUPS)),
            dma((3, GROUPS)),
            dma((GROUPS,)),
        ],
        compiler_params=pltpu.CompilerParams(
            collective_id=0, has_side_effects=True, vmem_limit_bytes=60 * 2**20
        ),
        name="memories",
    )(tokens, queries, log_decay.T, route_ids.T, gate_weights.T, kv_weight)


def solution(mesh):
    rows = P(("tm", "mem"), None)
    return jax.shard_map(
        on_device,
        mesh=mesh,
        in_specs=(rows, rows, rows, rows, rows, P("mem", None, None)),
        out_specs=rows,
        check_vma=False,
    )
```

```python
import functools

import jax
import jax.numpy as jnp
from jax import lax
from jax.experimental import pallas as pl
from jax.experimental.pallas import tpu as pltpu
from jax.sharding import PartitionSpec as P

MESH = pl.DeviceIdType.MESH
F32, BF16 = jnp.float32, jnp.bfloat16

MEM_Y, MEM_Z = 4, 4
MEMBERS = MEM_Y * MEM_Z
TM = 8
TOK = 256
CAP = 48
ROWS = MEMBERS * CAP
D = 2048
H = 16
HD = 128
XW = D + 128
CHUNK = 256
CHUNKS = ROWS // CHUNK
GROUPS = 4
GW = D // GROUPS
GH = H // GROUPS
PAIRS = H // 2
GP = PAIRS // GROUPS

SHIFTS = (
    (2, 2), (0, 2), (2, 0), (3, 2), (1, 2),
    (2, 3), (2, 1), (3, 1), (1, 3), (3, 3),
    (3, 0), (0, 3), (0, 1), (1, 1), (1, 0),
)
PEERS = len(SHIFTS)
BACK = 3


def mm(a, b, da=1, db=0):
    return lax.dot_general(a, b, (((da,), (db,)), ((), ())), preferred_element_type=F32)


def kernel(
    tok_hbm, qry_hbm, dec_ref, route_ref, gate_ref, w_hbm, out_hbm,
    tok, qry, w, onehot, chi, clo,
    sendx, recvx, sendq, recvq, kb, vb, osend, ret, outb,
    rcol, rrow, ends, atot, aprev, ub, inc, exc, ssend, srecv,
    load_sem, xs, xr, qs, qr, os_, or_, as_, ar, ss, sr, out_sem,
):
    tm = lax.axis_index("tm")
    me = lax.axis_index("mem")
    my, mz = lax.div(me, MEM_Z), lax.rem(me, MEM_Z)

    def at(dy, dz):
        return lax.rem(my + dy, MEM_Y) * MEM_Z + lax.rem(mz + dz, MEM_Z)

    core = lax.rem(tm, 2)
    turned = [(dy + core * (dz - dy), dz + core * (dy - dz)) for dy, dz in SHIFTS]
    to = [at(dy, dz) for dy, dz in turned]
    source = [at(MEM_Y - dy, MEM_Z - dz) for dy, dz in turned]

    def block(place):
        return pl.ds(pl.multiple_of(place * CAP, 16), CAP)

    barrier = pltpu.get_barrier_semaphore()
    for i in range(PEERS):
        pl.semaphore_signal(barrier, inc=1, device_id=(tm, to[i]), device_id_type=MESH)
    for d in range(1, TM):
        pl.semaphore_signal(
            barrier, inc=1, device_id=(lax.rem(tm + d, TM), me), device_id_type=MESH
        )

    load_tok = pltpu.make_async_copy(tok_hbm, tok, load_sem.at[0])
    load_qry = pltpu.make_async_copy(qry_hbm, qry, load_sem.at[1])
    load_w = pltpu.make_async_copy(w_hbm.at[0], w, load_sem.at[2])
    load_tok.start()
    load_qry.start()
    load_w.start()

    r0, r1 = route_ref[0:1, :], route_ref[1:2, :]
    mem_row = lax.broadcasted_iota(jnp.int32, (MEMBERS, TOK), 0)
    hot0 = (mem_row == r0).astype(F32)
    hot1 = (mem_row == r1).astype(F32)
    ahead = (
        lax.broadcasted_iota(jnp.int32, (TOK, TOK), 0)
        < lax.broadcasted_iota(jnp.int32, (TOK, TOK), 1)
    ).astype(BF16)
    rank = mm((hot0 + hot1).astype(BF16), ahead)
    slot0 = r0 * CAP + jnp.sum(hot0 * rank, axis=0, keepdims=True).astype(jnp.int32)
    slot1 = r1 * CAP + jnp.sum(hot1 * rank, axis=0, keepdims=True).astype(jnp.int32)
    slot_row = lax.broadcasted_iota(jnp.int32, (ROWS, TOK), 0)
    is0, is1 = slot_row == slot0, slot_row == slot1
    onehot[...] = (is0.astype(F32) + is1.astype(F32)).astype(BF16)

    for r in range(3):

        @pl.when(tm < (1 << r))
        def _():
            srecv[r] = jnp.zeros((H, HD, HD), BF16)

    for d in range(1, BACK + 1):

        @pl.when(tm < d)
        def _():
            aprev[d - 1] = jnp.zeros((H, HD), F32)

    dec_wide = jnp.concatenate([dec_ref[...], jnp.zeros((128 - H, TOK), BF16)], axis=0)
    sendx[:, D:XW] = mm(onehot[...], dec_wide, 1, 1).astype(BF16)
    load_tok.wait()

    def gather_x(j, c):
        cols = pl.ds(pl.multiple_of(j * 256, 256), 256)
        sendx[:, cols] = mm(onehot[...], tok[:, cols]).astype(BF16)
        return c

    lax.fori_loop(0, D // 256, gather_x, 0)
    pl.semaphore_wait(barrier, PEERS + TM - 1)

    def x_copy(i, src, dst):
        return pltpu.make_async_remote_copy(
            src_ref=sendx.at[block(src)],
            dst_ref=recvx.at[block(dst)],
            send_sem=xs.at[i],
            recv_sem=xr.at[i],
            device_id=(tm, to[i]),
            device_id_type=MESH,
        )

    def q_copy(g, i, src, dst):
        return pltpu.make_async_remote_copy(
            src_ref=sendq.at[g, block(src)],
            dst_ref=recvq.at[g, block(dst)],
            send_sem=qs.at[g, i],
            recv_sem=qr.at[g, i],
            device_id=(tm, to[i]),
            device_id_type=MESH,
        )

    def o_copy(g, i, src, dst):
        return pltpu.make_async_remote_copy(
            src_ref=osend.at[g, block(src)],
            dst_ref=ret.at[g, block(dst)],
            send_sem=os_.at[g, i],
            recv_sem=or_.at[g, i],
            device_id=(tm, to[i]),
            device_id_type=MESH,
        )

    def a_copy(d):
        return pltpu.make_async_remote_copy(
            src_ref=atot,
            dst_ref=aprev.at[d - 1],
            send_sem=as_.at[d - 1],
            recv_sem=ar.at[d - 1],
            device_id=(lax.rem(tm + d, TM), me),
            device_id_type=MESH,
        )

    def s_copy(r, g):
        heads = pl.ds(g * GH, GH)
        return pltpu.make_async_remote_copy(
            src_ref=ssend.at[r, heads],
            dst_ref=srecv.at[r, heads],
            send_sem=ss.at[r, g],
            recv_sem=sr.at[r, g],
            device_id=(lax.rem(tm + (1 << r), TM), me),
            device_id_type=MESH,
        )

    for i in range(PEERS):
        x_copy(i, to[i], me).start()

    load_qry.wait()

    def gather_q(g, c):
        for half in range(GW // 256):
            cols = pl.ds(pl.multiple_of(g * GW + half * 256, 256), 256)
            sendq[g, :, half * 256 : half * 256 + 256] = mm(onehot[...], qry[:, cols]).astype(BF16)
        for i in range(PEERS):
            q_copy(g, i, to[i], me).start()
        recvq[g, block(me), :] = sendq[g, block(me), :]
        return c

    lax.fori_loop(0, GROUPS, gather_q, 0)
    recvx[block(me), :] = sendx[block(me), :]

    gates = jnp.where(is0, gate_ref[0:1, :], 0.0) + jnp.where(is1, gate_ref[1:2, :], 0.0)
    gates_hi = gates.astype(BF16)
    chi[...] = gates_hi.T
    clo[...] = (gates - gates_hi.astype(F32)).astype(BF16).T

    load_w.wait()
    for i in range(PEERS):
        x_copy(i, to[i], source[i]).wait_recv()

    tri_r = lax.broadcasted_iota(jnp.int32, (CHUNK, CHUNK), 0)
    tri_c = lax.broadcasted_iota(jnp.int32, (CHUNK, CHUNK), 1)
    lower = (tri_r >= tri_c).astype(BF16)
    total = jnp.zeros((H, HD), F32)
    for c in range(CHUNKS):
        logs = recvx[c * CHUNK : (c + 1) * CHUNK, D:XW]
        rcol[c] = mm(lower, logs)
        rows = mm(logs, lower, 0, 1)[:H]
        rrow[c] = rows
        end = jnp.broadcast_to(rows[:, CHUNK - 1 : CHUNK], (H, HD))
        ends[c] = end
        total = total + end
    atot[...] = total
    for d in range(1, BACK + 1):

        @pl.when(tm + d < TM)
        def _():
            a_copy(d).start()

    lane = lax.broadcasted_iota(jnp.int32, (CHUNK, HD), 1)

    def column(c, h):
        return jnp.sum(jnp.where(lane == h, rcol[c], 0.0), axis=1, keepdims=True)

    def project(j, carry):
        kcols = pl.ds(pl.multiple_of(j * 256, 256), 256)
        vcols = pl.ds(pl.multiple_of(D + j * 256, 256), 256)
        kb[j] = mm(recvx[:, :D], w[:, kcols]).astype(BF16)
        vb[j] = mm(recvx[:, :D], w[:, vcols]).astype(BF16)
        for hh in range(2):
            h = 2 * j + hh
            lanes = slice(hh * HD, hh * HD + HD)
            local = None
            for c in range(CHUNKS):
                rows = slice(c * CHUNK, (c + 1) * CHUNK)
                end = ends[c, pl.ds(h, 1), :]
                fade = jnp.exp(end - column(c, h))
                keys = (kb[j, rows, lanes].astype(F32) * fade).astype(BF16)
                part = mm(keys, vb[j, rows, lanes], 0, 0)
                if c < CHUNKS - 1:
                    ub[c, h] = part
                local = part if c == 0 else jnp.exp(end) * local + part
            inc[h] = local
            ssend[0, h] = local.astype(BF16)
        return carry

    def gain(h, first, last):
        span = aprev[first, pl.ds(h, 1), :]
        for d in range(first + 1, last):
            span = span + aprev[d, pl.ds(h, 1), :]
        return span

    def round0(h, carry):
        got = srecv[0, h].astype(F32)
        exc[h] = got
        new = jnp.exp(atot[pl.ds(h, 1), :]) * got + inc[h]
        inc[h] = new
        ssend[1, h] = new.astype(BF16)
        return carry

    def round1(h, carry):
        got = srecv[1, h].astype(F32)
        before = gain(h, 0, 1)
        exc[h] = jnp.exp(before) * got + exc[h]
        new = jnp.exp(before + atot[pl.ds(h, 1), :]) * got + inc[h]
        ssend[2, h] = new.astype(BF16)
        return carry

    def round2(h, carry):
        got = srecv[2, h].astype(F32)
        exc[h] = jnp.exp(gain(h, 0, 3)) * got + exc[h]
        return carry

    def send_state(r, g):
        @pl.when(tm + (1 << r) < TM)
        def _():
            s_copy(r, g).start()

    def take_state(r, g):
        @pl.when(tm >= (1 << r))
        def _():
            s_copy(r, g).wait_recv()

    def stage(s, carry):
        @pl.when(s < GROUPS)
        def _():
            lax.fori_loop(s * GP, (s + 1) * GP, project, 0)
            send_state(0, s)

        @pl.when(s == 0)
        def _():
            for d in range(1, BACK + 1):

                @pl.when(tm >= d)
                def _():
                    a_copy(d).wait_recv()

        for r, step in enumerate((round0, round1, round2)):
            g = s - 1 - r

            @pl.when(jnp.logical_and(g >= 0, g < GROUPS))
            def _():
                take_state(r, g)
                lax.fori_loop(g * GH, (g + 1) * GH, step, 0)
                if r < 2:
                    send_state(r + 1, g)

        return carry

    lax.fori_loop(0, GROUPS + 3, stage, 0)

    def emit(g, carry):
        for i in range(PEERS):
            q_copy(g, i, to[i], source[i]).wait_recv()

        def head(hh, inner):
            h = g * GH + hh
            j = lax.div(h, 2)
            klanes = pl.ds(pl.multiple_of(lax.rem(h, 2) * HD, HD), HD)
            qlanes = pl.ds(pl.multiple_of(hh * HD, HD), HD)
            state = exc[h]
            for c in range(CHUNKS):
                rows = slice(c * CHUNK, (c + 1) * CHUNK)
                q = recvq[g, rows, qlanes]
                k = kb[j, rows, klanes]
                v = vb[j, rows, klanes]
                col = column(c, h)
                spread = jnp.exp(jnp.minimum(col - rrow[c, pl.ds(h, 1), :], 0.0))
                scores = jnp.where(tri_r >= tri_c, mm(q, k, 1, 1) * spread, 0.0)
                o = mm(scores.astype(BF16), v) + mm(q, state.astype(BF16)) * jnp.exp(col)
                scale = lax.rsqrt(jnp.mean(o * o, axis=1, keepdims=True) + 1e-06)
                osend[g, rows, qlanes] = (o * scale).astype(BF16)
                if c < CHUNKS - 1:
                    state = jnp.exp(ends[c, pl.ds(h, 1), :]) * state + ub[c, h]
            return inner

        lax.fori_loop(0, GH, head, 0)
        for i in range(PEERS):
            o_copy(g, i, to[i], me).start()
        ret[g, block(me), :] = osend[g, block(me), :]
        return carry

    lax.fori_loop(0, GROUPS, emit, 0)

    def out_copy(g):
        cols = pl.ds(pl.multiple_of(g * GW, GW), GW)
        return pltpu.make_async_copy(outb.at[:, cols], out_hbm.at[:, cols], out_sem.at[g])

    def finish(g, carry):
        for i in range(PEERS):
            o_copy(g, i, to[i], source[i]).wait_recv()
        for half in range(GW // 256):
            cols = slice(half * 256, half * 256 + 256)
            where = pl.ds(pl.multiple_of(g * GW + half * 256, 256), 256)
            got = ret[g, :, cols]
            outb[:, where] = (mm(chi[...], got) + mm(clo[...], got)).astype(BF16)
        out_copy(g).start()
        return carry

    lax.fori_loop(0, GROUPS, finish, 0)

    for i in range(PEERS):
        x_copy(i, to[i], me).wait_send()

    def sent(g, carry):
        for i in range(PEERS):
            q_copy(g, i, to[i], me).wait_send()
            o_copy(g, i, to[i], me).wait_send()
        for r in range(3):

            @pl.when(tm + (1 << r) < TM)
            def _():
                s_copy(r, g).wait_send()

        out_copy(g).wait()
        return carry

    lax.fori_loop(0, GROUPS, sent, 0)
    for d in range(1, BACK + 1):

        @pl.when(tm + d < TM)
        def _():
            a_copy(d).wait_send()


def on_device(tokens, queries, log_decay, route_ids, gate_weights, kv_weight):
    anywhere = pl.BlockSpec(memory_space=pl.ANY)
    near = pl.BlockSpec(memory_space=pltpu.VMEM)
    dma = pltpu.SemaphoreType.DMA
    return pl.pallas_call(
        kernel,
        out_shape=jax.ShapeDtypeStruct((TOK, D), BF16),
        in_specs=[anywhere, anywhere, near, near, near, anywhere],
        out_specs=anywhere,
        scratch_shapes=[
            pltpu.VMEM((TOK, D), BF16),
            pltpu.VMEM((TOK, D), BF16),
            pltpu.VMEM((D, 2 * D), BF16),
            pltpu.VMEM((ROWS, TOK), BF16),
            pltpu.VMEM((TOK, ROWS), BF16),
            pltpu.VMEM((TOK, ROWS), BF16),
            pltpu.VMEM((ROWS, XW), BF16),
            pltpu.VMEM((ROWS, XW), BF16),
            pltpu.VMEM((GROUPS, ROWS, GW), BF16),
            pltpu.VMEM((GROUPS, ROWS, GW), BF16),
            pltpu.VMEM((PAIRS, ROWS, 256), BF16),
            pltpu.VMEM((PAIRS, ROWS, 256), BF16),
            pltpu.VMEM((GROUPS, ROWS, GW), BF16),
            pltpu.VMEM((GROUPS, ROWS, GW), BF16),
            pltpu.VMEM((TOK, D), BF16),
            pltpu.VMEM((CHUNKS, CHUNK, HD), F32),
            pltpu.VMEM((CHUNKS, H, CHUNK), F32),
            pltpu.VMEM((CHUNKS, H, HD), F32),
            pltpu.VMEM((H, HD), F32),
            pltpu.VMEM((BACK, H, HD), F32),
            pltpu.VMEM((CHUNKS - 1, H, HD, HD), F32),
            pltpu.VMEM((H, HD, HD), F32),
            pltpu.VMEM((H, HD, HD), F32),
            pltpu.VMEM((3, H, HD, HD), BF16),
            pltpu.VMEM((3, H, HD, HD), BF16),
            dma((3,)),
            dma((PEERS,)),
            dma((PEERS,)),
            dma((GROUPS, PEERS)),
            dma((GROUPS, PEERS)),
            dma((GROUPS, PEERS)),
            dma((GROUPS, PEERS)),
            dma((BACK,)),
            dma((BACK,)),
            dma((3, GROUPS)),
            dma((3, GROUPS)),
            dma((GROUPS,)),
        ],
        compiler_params=pltpu.CompilerParams(
            collective_id=0, has_side_effects=True, vmem_limit_bytes=60 * 2**20
        ),
        name="memories",
    )(tokens, queries, log_decay.T, route_ids.T, gate_weights.T, kv_weight)


def solution(mesh):
    rows = P(("tm", "mem"), None)
    return jax.shard_map(
        on_device,
        mesh=mesh,
        in_specs=(rows, rows, rows, rows, rows, P("mem", None, None)),
        out_specs=rows,
        check_vma=False,
    )
```

```python
import functools

import jax
import jax.numpy as jnp
from jax import lax
from jax.experimental import pallas as pl
from jax.experimental.pallas import tpu as pltpu
from jax.sharding import PartitionSpec as P

MESH = pl.DeviceIdType.MESH
F32, BF16 = jnp.float32, jnp.bfloat16

MEM_Y, MEM_Z = 4, 4
MEMBERS = MEM_Y * MEM_Z
TM = 8
TOK = 256
CAP = 48
ROWS = MEMBERS * CAP
D = 2048
H = 16
HD = 128
XW = D + 128
CHUNK = 256
CHUNKS = ROWS // CHUNK
GROUPS = 4
GW = D // GROUPS
GH = H // GROUPS
PAIRS = H // 2
GP = PAIRS // GROUPS

SHIFTS = (
    (2, 2), (0, 2), (2, 0), (3, 2), (1, 2),
    (2, 3), (2, 1), (3, 1), (1, 3), (3, 3),
    (3, 0), (0, 3), (0, 1), (1, 1), (1, 0),
)
PEERS = len(SHIFTS)
BACK = 3


def mm(a, b, da=1, db=0):
    return lax.dot_general(a, b, (((da,), (db,)), ((), ())), preferred_element_type=F32)


def split(a):
    high = a.astype(BF16)
    return high, (a - high.astype(F32)).astype(BF16)


def kernel(
    tok_hbm, qry_hbm, dec_ref, route_ref, gate_ref, w_hbm, out_hbm,
    tok, qry, w, onehot, chi, clo,
    sendx, recvx, sendq, recvq, kb, vb, osend, ret, outb,
    rcol, rrow, ends, atot, aprev, ub, inc, exc, ssend, srecv,
    load_sem, xs, xr, qs, qr, os_, or_, as_, ar, ss, sr, out_sem,
):
    tm = lax.axis_index("tm")
    me = lax.axis_index("mem")
    my, mz = lax.div(me, MEM_Z), lax.rem(me, MEM_Z)

    def at(dy, dz):
        return lax.rem(my + dy, MEM_Y) * MEM_Z + lax.rem(mz + dz, MEM_Z)

    core = lax.rem(tm, 2)
    turned = [(dy + core * (dz - dy), dz + core * (dy - dz)) for dy, dz in SHIFTS]
    to = [at(dy, dz) for dy, dz in turned]

    def block(place):
        return pl.ds(pl.multiple_of(place * CAP, 16), CAP)

    load_tok = pltpu.make_async_copy(tok_hbm, tok, load_sem.at[0])
    load_qry = pltpu.make_async_copy(qry_hbm, qry, load_sem.at[1])
    load_w = pltpu.make_async_copy(w_hbm.at[0], w, load_sem.at[2])
    load_tok.start()

    barrier = pltpu.get_barrier_semaphore()
    for i in range(PEERS):
        pl.semaphore_signal(barrier, inc=1, device_id=(tm, to[i]), device_id_type=MESH)
    for d in range(1, TM):
        pl.semaphore_signal(
            barrier, inc=1, device_id=(lax.rem(tm + d, TM), me), device_id_type=MESH
        )

    r0, r1 = route_ref[0:1, :], route_ref[1:2, :]
    mem_row = lax.broadcasted_iota(jnp.int32, (MEMBERS, TOK), 0)
    hot0 = (mem_row == r0).astype(F32)
    hot1 = (mem_row == r1).astype(F32)
    ahead = (
        lax.broadcasted_iota(jnp.int32, (TOK, TOK), 0)
        < lax.broadcasted_iota(jnp.int32, (TOK, TOK), 1)
    ).astype(BF16)
    rank = mm((hot0 + hot1).astype(BF16), ahead)
    slot0 = r0 * CAP + jnp.sum(hot0 * rank, axis=0, keepdims=True).astype(jnp.int32)
    slot1 = r1 * CAP + jnp.sum(hot1 * rank, axis=0, keepdims=True).astype(jnp.int32)
    slot_row = lax.broadcasted_iota(jnp.int32, (ROWS, TOK), 0)
    is0, is1 = slot_row == slot0, slot_row == slot1
    onehot[...] = (is0.astype(F32) + is1.astype(F32)).astype(BF16)

    dec_wide = jnp.concatenate([dec_ref[...], jnp.zeros((128 - H, TOK), BF16)], axis=0)
    sendx[:, D:XW] = mm(onehot[...], dec_wide, 1, 1).astype(BF16)
    def x_copy(i, src, dst):
        return pltpu.make_async_remote_copy(
            src_ref=sendx.at[src],
            dst_ref=recvx.at[dst],
            send_sem=xs.at[0],
            recv_sem=xr.at[0],
            device_id=(tm, to[i]),
            device_id_type=MESH,
        )

    def q_copy(g, i, src, dst):
        return pltpu.make_async_remote_copy(
            src_ref=sendq.at[g, src],
            dst_ref=recvq.at[g, dst],
            send_sem=qs.at[g],
            recv_sem=qr.at[g],
            device_id=(tm, to[i]),
            device_id_type=MESH,
        )

    def o_copy(g, i, src, dst):
        return pltpu.make_async_remote_copy(
            src_ref=osend.at[g, src],
            dst_ref=ret.at[g, dst],
            send_sem=os_.at[g],
            recv_sem=or_.at[g],
            device_id=(tm, to[i]),
            device_id_type=MESH,
        )

    every = slice(0, PEERS * CAP)

    def a_copy(d):
        return pltpu.make_async_remote_copy(
            src_ref=atot,
            dst_ref=aprev.at[d - 1],
            send_sem=as_.at[d - 1],
            recv_sem=ar.at[d - 1],
            device_id=(lax.rem(tm + d, TM), me),
            device_id_type=MESH,
        )

    def s_copy(r, g):
        heads = pl.ds(g * GH, GH)
        return pltpu.make_async_remote_copy(
            src_ref=ssend.at[r, heads],
            dst_ref=srecv.at[r, heads],
            send_sem=ss.at[r, g],
            recv_sem=sr.at[r, g],
            device_id=(lax.rem(tm + (1 << r), TM), me),
            device_id_type=MESH,
        )

    load_tok.wait()
    pl.semaphore_wait(barrier, PEERS + TM - 1)
    for i in range(PEERS):
        rows = block(to[i])
        sendx[rows, :D] = mm(onehot[rows, :], tok[...]).astype(BF16)
        x_copy(i, rows, block(me)).start()
    load_qry.start()
    load_w.start()
    mine = block(me)
    recvx[mine, :D] = mm(onehot[mine, :], tok[...]).astype(BF16)
    recvx[mine, D:XW] = sendx[mine, D:XW]

    for r in range(3):

        @pl.when(tm < (1 << r))
        def _():
            srecv[r] = jnp.zeros((H, HD, HD), BF16)

    for d in range(1, BACK + 1):

        @pl.when(tm < d)
        def _():
            aprev[d - 1] = jnp.zeros((H, HD), F32)

    load_qry.wait()

    def gather_q(g, c):
        for half in range(GW // 256):
            cols = pl.ds(pl.multiple_of(g * GW + half * 256, 256), 256)
            sendq[g, :, half * 256 : half * 256 + 256] = mm(onehot[...], qry[:, cols]).astype(BF16)
        for i in range(PEERS):
            q_copy(g, i, block(to[i]), mine).start()
        recvq[g, mine, :] = sendq[g, mine, :]
        return c

    lax.fori_loop(0, GROUPS, gather_q, 0)

    gates = jnp.where(is0, gate_ref[0:1, :], 0.0) + jnp.where(is1, gate_ref[1:2, :], 0.0)
    gates_hi, gates_lo = split(gates)
    chi[...] = gates_hi.T
    clo[...] = gates_lo.T

    load_w.wait()
    x_copy(0, every, every).wait_recv()

    tri_r = lax.broadcasted_iota(jnp.int32, (CHUNK, CHUNK), 0)
    tri_c = lax.broadcasted_iota(jnp.int32, (CHUNK, CHUNK), 1)
    lower = (tri_r >= tri_c).astype(BF16)
    total = jnp.zeros((H, HD), F32)
    for c in range(CHUNKS):
        logs = recvx[c * CHUNK : (c + 1) * CHUNK, D:XW]
        rcol[c] = mm(lower, logs)
        rows = mm(logs, lower, 0, 1)[:H]
        rrow[c] = rows
        end = jnp.broadcast_to(rows[:, CHUNK - 1 : CHUNK], (H, HD))
        ends[c] = end
        total = total + end
    atot[...] = total
    for d in range(1, BACK + 1):

        @pl.when(tm + d < TM)
        def _():
            a_copy(d).start()

    lane = lax.broadcasted_iota(jnp.int32, (CHUNK, HD), 1)

    def column(c, h):
        return jnp.sum(jnp.where(lane == h, rcol[c], 0.0), axis=1, keepdims=True)

    def project(j, carry):
        kcols = pl.ds(pl.multiple_of(j * 256, 256), 256)
        vcols = pl.ds(pl.multiple_of(D + j * 256, 256), 256)
        kb[j] = mm(recvx[:, :D], w[:, kcols]).astype(BF16)
        vb[j] = mm(recvx[:, :D], w[:, vcols]).astype(BF16)
        for hh in range(2):
            h = 2 * j + hh
            lanes = slice(hh * HD, hh * HD + HD)
            local = None
            for c in range(CHUNKS):
                rows = slice(c * CHUNK, (c + 1) * CHUNK)
                end = ends[c, pl.ds(h, 1), :]
                fade = jnp.exp(end - column(c, h))
                keys = (kb[j, rows, lanes].astype(F32) * fade).astype(BF16)
                part = mm(keys, vb[j, rows, lanes], 0, 0)
                if c < CHUNKS - 1:
                    ub[c, h] = part
                local = part if c == 0 else jnp.exp(end) * local + part
            inc[h] = local
            ssend[0, h] = local.astype(BF16)
        return carry

    def gain(h, first, last):
        span = aprev[first, pl.ds(h, 1), :]
        for d in range(first + 1, last):
            span = span + aprev[d, pl.ds(h, 1), :]
        return span

    def round0(h, carry):
        got = srecv[0, h].astype(F32)
        exc[h] = got
        new = jnp.exp(atot[pl.ds(h, 1), :]) * got + inc[h]
        inc[h] = new
        ssend[1, h] = new.astype(BF16)
        return carry

    def round1(h, carry):
        got = srecv[1, h].astype(F32)
        before = gain(h, 0, 1)
        exc[h] = jnp.exp(before) * got + exc[h]
        new = jnp.exp(before + atot[pl.ds(h, 1), :]) * got + inc[h]
        ssend[2, h] = new.astype(BF16)
        return carry

    def round2(h, carry):
        got = srecv[2, h].astype(F32)
        exc[h] = jnp.exp(gain(h, 0, 3)) * got + exc[h]
        return carry

    def send_state(r, g):
        @pl.when(tm + (1 << r) < TM)
        def _():
            s_copy(r, g).start()

    def take_state(r, g):
        @pl.when(tm >= (1 << r))
        def _():
            s_copy(r, g).wait_recv()

    def emit(g):
        q_copy(g, 0, every, every).wait_recv()

        def head(hh, inner):
            h = g * GH + hh
            j = lax.div(h, 2)
            klanes = pl.ds(pl.multiple_of(lax.rem(h, 2) * HD, HD), HD)
            qlanes = pl.ds(pl.multiple_of(hh * HD, HD), HD)
            state = exc[h]
            for c in range(CHUNKS):
                rows = slice(c * CHUNK, (c + 1) * CHUNK)
                q = recvq[g, rows, qlanes]
                k = kb[j, rows, klanes]
                v = vb[j, rows, klanes]
                col = column(c, h)
                spread = jnp.exp(jnp.minimum(col - rrow[c, pl.ds(h, 1), :], 0.0))
                scores = jnp.where(tri_r >= tri_c, mm(q, k, 1, 1) * spread, 0.0)
                s_hi, s_lo = split(scores)
                t_hi, t_lo = split(state)
                o = mm(s_hi, v) + mm(s_lo, v) + (mm(q, t_hi) + mm(q, t_lo)) * jnp.exp(col)
                scale = lax.rsqrt(jnp.mean(o * o, axis=1, keepdims=True) + 1e-06)
                osend[g, rows, qlanes] = (o * scale).astype(BF16)
                if c < CHUNKS - 1:
                    state = jnp.exp(ends[c, pl.ds(h, 1), :]) * state + ub[c, h]
            return inner

        lax.fori_loop(0, GH, head, 0)
        for i in range(PEERS):
            o_copy(g, i, block(to[i]), mine).start()
        ret[g, mine, :] = osend[g, mine, :]

    def stage(s, carry):
        @pl.when(s < GROUPS)
        def _():
            lax.fori_loop(s * GP, (s + 1) * GP, project, 0)
            send_state(0, s)

        @pl.when(s == 0)
        def _():
            for d in range(1, BACK + 1):

                @pl.when(tm >= d)
                def _():
                    a_copy(d).wait_recv()

        for r, step in enumerate((round0, round1, round2)):
            g = s - 1 - r

            @pl.when(jnp.logical_and(g >= 0, g < GROUPS))
            def _():
                take_state(r, g)
                lax.fori_loop(g * GH, (g + 1) * GH, step, 0)
                if r < 2:
                    send_state(r + 1, g)
                else:
                    emit(g)

        return carry

    lax.fori_loop(0, GROUPS + 3, stage, 0)


    def out_copy(g):
        cols = pl.ds(pl.multiple_of(g * GW, GW), GW)
        return pltpu.make_async_copy(outb.at[:, cols], out_hbm.at[:, cols], out_sem.at[g])

    def finish(g, carry):
        o_copy(g, 0, every, every).wait_recv()
        for half in range(GW // 256):
            cols = slice(half * 256, half * 256 + 256)
            where = pl.ds(pl.multiple_of(g * GW + half * 256, 256), 256)
            got = ret[g, :, cols]
            outb[:, where] = (mm(chi[...], got) + mm(clo[...], got)).astype(BF16)
        out_copy(g).start()
        return carry

    lax.fori_loop(0, GROUPS, finish, 0)

    x_copy(0, every, every).wait_send()

    def sent(g, carry):
        q_copy(g, 0, every, every).wait_send()
        o_copy(g, 0, every, every).wait_send()
        for r in range(3):

            @pl.when(tm + (1 << r) < TM)
            def _():
                s_copy(r, g).wait_send()

        out_copy(g).wait()
        return carry

    lax.fori_loop(0, GROUPS, sent, 0)
    for d in range(1, BACK + 1):

        @pl.when(tm + d < TM)
        def _():
            a_copy(d).wait_send()


def on_device(tokens, queries, log_decay, route_ids, gate_weights, kv_weight):
    anywhere = pl.BlockSpec(memory_space=pl.ANY)
    near = pl.BlockSpec(memory_space=pltpu.VMEM)
    dma = pltpu.SemaphoreType.DMA
    return pl.pallas_call(
        kernel,
        out_shape=jax.ShapeDtypeStruct((TOK, D), BF16),
        in_specs=[anywhere, anywhere, near, near, near, anywhere],
        out_specs=anywhere,
        scratch_shapes=[
            pltpu.VMEM((TOK, D), BF16),
            pltpu.VMEM((TOK, D), BF16),
            pltpu.VMEM((D, 2 * D), BF16),
            pltpu.VMEM((ROWS, TOK), BF16),
            pltpu.VMEM((TOK, ROWS), BF16),
            pltpu.VMEM((TOK, ROWS), BF16),
            pltpu.VMEM((ROWS, XW), BF16),
            pltpu.VMEM((ROWS, XW), BF16),
            pltpu.VMEM((GROUPS, ROWS, GW), BF16),
            pltpu.VMEM((GROUPS, ROWS, GW), BF16),
            pltpu.VMEM((PAIRS, ROWS, 256), BF16),
            pltpu.VMEM((PAIRS, ROWS, 256), BF16),
            pltpu.VMEM((GROUPS, ROWS, GW), BF16),
            pltpu.VMEM((GROUPS, ROWS, GW), BF16),
            pltpu.VMEM((TOK, D), BF16),
            pltpu.VMEM((CHUNKS, CHUNK, HD), F32),
            pltpu.VMEM((CHUNKS, H, CHUNK), F32),
            pltpu.VMEM((CHUNKS, H, HD), F32),
            pltpu.VMEM((H, HD), F32),
            pltpu.VMEM((BACK, H, HD), F32),
            pltpu.VMEM((CHUNKS - 1, H, HD, HD), F32),
            pltpu.VMEM((H, HD, HD), F32),
            pltpu.VMEM((H, HD, HD), F32),
            pltpu.VMEM((3, H, HD, HD), BF16),
            pltpu.VMEM((3, H, HD, HD), BF16),
            dma((3,)),
            dma((1,)),
            dma((1,)),
            dma((GROUPS,)),
            dma((GROUPS,)),
            dma((GROUPS,)),
            dma((GROUPS,)),
            dma((BACK,)),
            dma((BACK,)),
            dma((3, GROUPS)),
            dma((3, GROUPS)),
            dma((GROUPS,)),
        ],
        compiler_params=pltpu.CompilerParams(
            collective_id=0, has_side_effects=True, vmem_limit_bytes=60 * 2**20
        ),
        name="memories",
    )(tokens, queries, log_decay.T, route_ids.T, gate_weights.T, kv_weight)


def solution(mesh):
    rows = P(("tm", "mem"), None)
    return jax.shard_map(
        on_device,
        mesh=mesh,
        in_specs=(rows, rows, rows, rows, rows, P("mem", None, None)),
        out_specs=rows,
        check_vma=False,
    )
```

```python
import functools

import jax
import jax.numpy as jnp
from jax import lax
from jax.experimental import pallas as pl
from jax.experimental.pallas import tpu as pltpu
from jax.sharding import PartitionSpec as P

MESH = pl.DeviceIdType.MESH
F32, BF16 = jnp.float32, jnp.bfloat16

MEM_Y, MEM_Z = 4, 4
MEMBERS = MEM_Y * MEM_Z
TM = 8
TOK = 256
CAP = 48
ROWS = MEMBERS * CAP
D = 2048
H = 16
HD = 128
CHUNK = 256
CHUNKS = ROWS // CHUNK
GROUPS = 4
GW = D // GROUPS
GH = H // GROUPS
PAIRS = H // 2
GP = PAIRS // GROUPS

SHIFTS = (
    (2, 2), (0, 2), (2, 0), (3, 2), (1, 2),
    (2, 3), (2, 1), (3, 1), (1, 3), (3, 3),
    (3, 0), (0, 3), (0, 1), (1, 1), (1, 0),
)
PEERS = len(SHIFTS)
HALF_SHIFTS = ((1, 2), (0, 2), (1, 1), (1, 3), (0, 1), (0, 3), (1, 0))
HALF = MEMBERS // 2
HALF_PEERS = len(HALF_SHIFTS)
QUARTERS = 4
QW = D // QUARTERS
BACK = 3


def mm(a, b, da=1, db=0):
    return lax.dot_general(a, b, (((da,), (db,)), ((), ())), preferred_element_type=F32)


def split(a):
    high = a.astype(BF16)
    return high, (a - high.astype(F32)).astype(BF16)


def kernel(
    tok_hbm, qry_hbm, dec_ref, route_ref, gate_ref, w_hbm, out_hbm,
    tok, qry, w, onehot, picks, chi, clo, slots, slotp, xp, qp,
    sendd, recvd, sendx, recvx, sendq, recvq, kb, vb, osend, ret, outb,
    rcol, rrow, ends, atot, aprev, ub, inc, exc, ssend, srecv,
    load_sem, sps, spr, xps, xpr, qps, qpr, ds_, dr,
    xs, xr, qs, qr, os_, or_, as_, ar, ss, sr, out_sem,
):
    tm = lax.axis_index("tm")
    me = lax.axis_index("mem")
    my, mz = lax.div(me, MEM_Z), lax.rem(me, MEM_Z)

    def at(dy, dz):
        return lax.rem(my + dy, MEM_Y) * MEM_Z + lax.rem(mz + dz, MEM_Z)

    core = lax.rem(tm, 2)
    turned = [(dy + core * (dz - dy), dz + core * (dy - dz)) for dy, dz in SHIFTS]
    to = [at(dy, dz) for dy, dz in turned]

    y_swap, y_flip = my + 1 - 2 * lax.rem(my, 2), MEM_Y - 1 - my
    z_swap, z_flip = mz + 1 - 2 * lax.rem(mz, 2), MEM_Z - 1 - mz
    partner = (
        y_swap * MEM_Z + mz,
        y_flip * MEM_Z + mz,
        my * MEM_Z + z_swap,
        my * MEM_Z + z_flip,
    )
    other = (y_flip, y_swap, z_flip, z_swap)

    def in_half(g, across, step):
        if g < 2:
            ring = lax.rem(mz + step, MEM_Z)
            return (other[g] if across else my) * MEM_Z + ring, across * 4 + ring
        ring = lax.rem(my + step, MEM_Y)
        return ring * MEM_Z + (other[g] if across else mz), across * 4 + ring

    def block(place):
        return pl.ds(pl.multiple_of(place * CAP, 16), CAP)

    load_tok = pltpu.make_async_copy(tok_hbm, tok, load_sem.at[0])
    load_qry = pltpu.make_async_copy(qry_hbm, qry, load_sem.at[1])
    load_w = pltpu.make_async_copy(w_hbm.at[0], w, load_sem.at[2])
    load_tok.start()
    load_qry.start()

    barrier = pltpu.get_barrier_semaphore()
    for i in range(PEERS):
        pl.semaphore_signal(barrier, inc=1, device_id=(tm, to[i]), device_id_type=MESH)
    for d in range(1, TM):
        pl.semaphore_signal(
            barrier, inc=1, device_id=(lax.rem(tm + d, TM), me), device_id_type=MESH
        )

    r0, r1 = route_ref[0:1, :], route_ref[1:2, :]
    mem_row = lax.broadcasted_iota(jnp.int32, (MEMBERS, TOK), 0)
    hot0 = (mem_row == r0).astype(F32)
    hot1 = (mem_row == r1).astype(F32)
    ahead = (
        lax.broadcasted_iota(jnp.int32, (TOK, TOK), 0)
        < lax.broadcasted_iota(jnp.int32, (TOK, TOK), 1)
    ).astype(BF16)
    rank = mm((hot0 + hot1).astype(BF16), ahead)
    slot0 = r0.astype(F32) * CAP + jnp.sum(hot0 * rank, axis=0, keepdims=True)
    slot1 = r1.astype(F32) * CAP + jnp.sum(hot1 * rank, axis=0, keepdims=True)
    slots[...] = jnp.concatenate([slot0, slot1, jnp.zeros((6, TOK), F32)], axis=0)
    slot_row = lax.broadcasted_iota(jnp.int32, (ROWS + 128, TOK), 0).astype(F32)
    is0, is1 = slot_row == slot0, slot_row == slot1
    onehot[...] = (is0.astype(F32) + is1.astype(F32)).astype(BF16)

    def gather_d(e, c):
        rows = onehot[pl.ds(pl.multiple_of(e * CAP, 16), 128), :]
        sendd[e] = mm(dec_ref[...], rows, 1, 1).astype(BF16)
        return c

    def slot_copy(g):
        return pltpu.make_async_remote_copy(
            src_ref=slots,
            dst_ref=slotp.at[g],
            send_sem=sps.at[0],
            recv_sem=spr.at[g],
            device_id=(tm, partner[g]),
            device_id_type=MESH,
        )

    def xp_copy(g):
        return pltpu.make_async_remote_copy(
            src_ref=tok_hbm.at[:, g * QW : (g + 1) * QW],
            dst_ref=xp.at[g],
            send_sem=xps.at[0],
            recv_sem=xpr.at[g],
            device_id=(tm, partner[g]),
            device_id_type=MESH,
        )

    def qp_copy(g, u):
        first = (u * QUARTERS + g) * 256
        return pltpu.make_async_remote_copy(
            src_ref=qry_hbm.at[:, first : first + 256],
            dst_ref=qp.at[g, u],
            send_sem=qps.at[0],
            recv_sem=qpr.at[g],
            device_id=(tm, partner[g]),
            device_id_type=MESH,
        )

    def whole(ref, send_sem, recv_sem):
        return pltpu.make_async_remote_copy(
            src_ref=ref,
            dst_ref=ref,
            send_sem=send_sem,
            recv_sem=recv_sem,
            device_id=(tm, to[0]),
            device_id_type=MESH,
        )

    def d_copy(i):
        return pltpu.make_async_remote_copy(
            src_ref=sendd.at[to[i]],
            dst_ref=recvd.at[me],
            send_sem=ds_.at[0],
            recv_sem=dr.at[0],
            device_id=(tm, to[i]),
            device_id_type=MESH,
        )

    def x_copy(g, own, src, dst, place):
        return pltpu.make_async_remote_copy(
            src_ref=sendx.at[g, own, src],
            dst_ref=recvx.at[dst, g * QW : (g + 1) * QW],
            send_sem=xs.at[g],
            recv_sem=xr.at[g],
            device_id=(tm, place),
            device_id_type=MESH,
        )

    def q_copy(j, own, src, dst, place):
        return pltpu.make_async_remote_copy(
            src_ref=sendq.at[j, own, src],
            dst_ref=recvq.at[j, dst],
            send_sem=qs.at[j],
            recv_sem=qr.at[j],
            device_id=(tm, place),
            device_id_type=MESH,
        )

    def o_copy(g, i, src, dst):
        return pltpu.make_async_remote_copy(
            src_ref=osend.at[g, src],
            dst_ref=ret.at[g, dst],
            send_sem=os_.at[g],
            recv_sem=or_.at[g],
            device_id=(tm, to[i]),
            device_id_type=MESH,
        )

    every = slice(0, PEERS * CAP)
    half_every = slice(0, 2 * HALF_PEERS * CAP)

    def a_copy(d):
        return pltpu.make_async_remote_copy(
            src_ref=atot,
            dst_ref=aprev.at[d - 1],
            send_sem=as_.at[d - 1],
            recv_sem=ar.at[d - 1],
            device_id=(lax.rem(tm + d, TM), me),
            device_id_type=MESH,
        )

    def s_copy(r, g):
        heads = pl.ds(g * GH, GH)
        return pltpu.make_async_remote_copy(
            src_ref=ssend.at[r, heads],
            dst_ref=srecv.at[r, heads],
            send_sem=ss.at[r],
            recv_sem=sr.at[r, g],
            device_id=(lax.rem(tm + (1 << r), TM), me),
            device_id_type=MESH,
        )

    pl.semaphore_wait(barrier, PEERS + TM - 1)
    for g in range(QUARTERS):
        slot_copy(g).start()
    for g in range(QUARTERS):
        xp_copy(g).start()
    lax.fori_loop(0, MEMBERS, gather_d, 0)
    for i in range(PEERS):
        d_copy(i).start()
    for u in range(2):
        for g in range(QUARTERS):
            qp_copy(g, u).start()
    recvd[me] = sendd[me]

    pick_row = lax.broadcasted_iota(jnp.int32, (HALF * CAP, TOK), 0)
    over = (pick_row >= HALF * CAP // 2).astype(jnp.int32)
    ring_row = pick_row - over * (HALF * CAP // 2)
    ring = sum((ring_row >= k * CAP).astype(jnp.int32) for k in range(1, 4))

    def wanted(g):
        if g < 2:
            return (ring_row + (my + over * (other[g] - my)) * (MEM_Z * CAP)).astype(F32)
        column_slot = (mz + over * (other[g] - mz)) * CAP
        return (ring_row + ring * ((MEM_Z - 1) * CAP) + column_slot).astype(F32)

    def pick(g, slots_now):
        goal = wanted(g)
        first, second = goal == slots_now[0:1, :], goal == slots_now[1:2, :]
        return (first.astype(F32) + second.astype(F32)).astype(BF16)

    load_tok.wait()
    for g in range(QUARTERS):
        picks[g, 0] = pick(g, slots[...])
        sendx[g, 0] = mm(picks[g, 0], tok[:, g * QW : (g + 1) * QW]).astype(BF16)
    for g in range(QUARTERS):
        slot_copy(g).wait_recv()
        picks[g, 1] = pick(g, slotp[g])
    for g in range(QUARTERS):
        whole(xp.at[g], xps.at[0], xpr.at[g]).wait_recv()
        sendx[g, 1] = mm(picks[g, 1], xp[g]).astype(BF16)
    mine = block(me)
    for across, step in HALF_SHIFTS:
        for g in range(QUARTERS):
            place, number = in_half(g, across, step)
            for own in range(2):
                dst = block(partner[g]) if own else mine
                x_copy(g, own, block(number), dst, place).start()
    load_w.start()
    for g in range(QUARTERS):
        number = in_half(g, 0, 0)[1]
        cols = slice(g * QW, (g + 1) * QW)
        recvx[mine, cols] = sendx[g, 0, block(number), :]
        recvx[block(partner[g]), cols] = sendx[g, 1, block(number), :]

    load_qry.wait()
    for g in range(QUARTERS):
        whole(qp.at[g], qps.at[0], qpr.at[g]).wait_recv()

    def gather_q(u, c):
        for g in range(QUARTERS):
            j = u * QUARTERS + g
            cols = pl.ds(pl.multiple_of(j * 256, 256), 256)
            sendq[j, 0] = mm(picks[g, 0], qry[:, cols]).astype(BF16)
            sendq[j, 1] = mm(picks[g, 1], qp[g, u]).astype(BF16)
        for across, step in HALF_SHIFTS:
            for g in range(QUARTERS):
                place, number = in_half(g, across, step)
                j = u * QUARTERS + g
                for own in range(2):
                    dst = block(partner[g]) if own else mine
                    q_copy(j, own, block(number), dst, place).start()
        for g in range(QUARTERS):
            j = u * QUARTERS + g
            number = in_half(g, 0, 0)[1]
            recvq[j, mine, :] = sendq[j, 0, block(number), :]
            recvq[j, block(partner[g]), :] = sendq[j, 1, block(number), :]
        return c

    lax.fori_loop(0, 2, gather_q, 0)

    for r in range(3):

        @pl.when(tm < (1 << r))
        def _():
            srecv[r] = jnp.zeros((H, HD, HD), BF16)

    for d in range(1, BACK + 1):

        @pl.when(tm < d)
        def _():
            aprev[d - 1] = jnp.zeros((H, HD), F32)

    gates = jnp.where(is0, gate_ref[0:1, :], 0.0) + jnp.where(is1, gate_ref[1:2, :], 0.0)
    gates = gates[:ROWS]
    gates_hi, gates_lo = split(gates)
    chi[...] = gates_hi.T
    clo[...] = gates_lo.T

    whole(recvd.at[0:PEERS], ds_.at[0], dr.at[0]).wait_recv()
    tri_r = lax.broadcasted_iota(jnp.int32, (CHUNK, CHUNK), 0)
    tri_c = lax.broadcasted_iota(jnp.int32, (CHUNK, CHUNK), 1)
    place_row = lax.broadcasted_iota(jnp.int32, (128, CHUNK), 0)
    place_col = lax.broadcasted_iota(jnp.int32, (128, CHUNK), 1)
    used = place_row < CAP

    def add_logs(src, sums):
        at_row = place_row + src * CAP
        out = []
        for c in range(CHUNKS):
            within = jnp.logical_and(at_row >= c * CHUNK, at_row <= place_col + c * CHUNK)
            take = jnp.where(jnp.logical_and(used, within), 1.0, 0.0).astype(BF16)
            out.append(sums[c] + mm(recvd[src], take))
        return tuple(out)

    sums = lax.fori_loop(
        0, MEMBERS, add_logs, tuple(jnp.zeros((H, CHUNK), F32) for c in range(CHUNKS))
    )
    total = jnp.zeros((H, HD), F32)
    for c in range(CHUNKS):
        rows = sums[c]
        rrow[c] = rows
        rcol[c] = jnp.concatenate([rows, jnp.zeros((HD - H, CHUNK), F32)], axis=0).T
        end = jnp.broadcast_to(rows[:, CHUNK - 1 : CHUNK], (H, HD))
        ends[c] = end
        total = total + end
    atot[...] = total
    for d in range(1, BACK + 1):

        @pl.when(tm + d < TM)
        def _():
            a_copy(d).start()

    load_w.wait()
    for g in range(QUARTERS):
        x_copy(g, 0, slice(0, CAP), half_every, to[0]).wait_recv()

    lane = lax.broadcasted_iota(jnp.int32, (CHUNK, HD), 1)

    def column(c, h):
        return jnp.sum(jnp.where(lane == h, rcol[c], 0.0), axis=1, keepdims=True)

    def project(j, carry):
        def columns(first):
            cols = pl.ds(pl.multiple_of(first, 256), 256)
            return mm(recvx[...], w[:, cols]).astype(BF16)

        kb[j] = columns(j * 256)
        vb[j] = columns(D + j * 256)
        for hh in range(2):
            h = 2 * j + hh
            lanes = slice(hh * HD, hh * HD + HD)
            local = None
            for c in range(CHUNKS):
                rows = slice(c * CHUNK, (c + 1) * CHUNK)
                end = ends[c, pl.ds(h, 1), :]
                fade = jnp.exp(end - column(c, h))
                keys = (kb[j, rows, lanes].astype(F32) * fade).astype(BF16)
                part = mm(keys, vb[j, rows, lanes], 0, 0)
                if c < CHUNKS - 1:
                    ub[c, h] = part
                local = part if c == 0 else jnp.exp(end) * local + part
            inc[h] = local
            ssend[0, h] = local.astype(BF16)
        return carry

    def gain(h, first, last):
        span = aprev[first, pl.ds(h, 1), :]
        for d in range(first + 1, last):
            span = span + aprev[d, pl.ds(h, 1), :]
        return span

    def round0(h, carry):
        got = srecv[0, h].astype(F32)
        exc[h] = got
        new = jnp.exp(atot[pl.ds(h, 1), :]) * got + inc[h]
        inc[h] = new
        ssend[1, h] = new.astype(BF16)
        return carry

    def round1(h, carry):
        got = srecv[1, h].astype(F32)
        before = gain(h, 0, 1)
        exc[h] = jnp.exp(before) * got + exc[h]
        new = jnp.exp(before + atot[pl.ds(h, 1), :]) * got + inc[h]
        ssend[2, h] = new.astype(BF16)
        return carry

    def round2(h, carry):
        got = srecv[2, h].astype(F32)
        exc[h] = jnp.exp(gain(h, 0, 3)) * got + exc[h]
        return carry

    def send_state(r, g):
        @pl.when(tm + (1 << r) < TM)
        def _():
            s_copy(r, g).start()

    def take_state(r, g):
        @pl.when(tm >= (1 << r))
        def _():
            s_copy(r, g).wait_recv()

    def emit(g):
        for p in range(2):
            q_copy(2 * g + p, 0, slice(0, CAP), half_every, to[0]).wait_recv()

        def head(hh, inner):
            h = g * GH + hh
            j = lax.div(h, 2)
            klanes = pl.ds(pl.multiple_of(lax.rem(h, 2) * HD, HD), HD)
            qlanes = pl.ds(pl.multiple_of(hh * HD, HD), HD)
            state = exc[h]
            for c in range(CHUNKS):
                rows = slice(c * CHUNK, (c + 1) * CHUNK)
                q = recvq[j, rows, klanes]
                k = kb[j, rows, klanes]
                v = vb[j, rows, klanes]
                col = column(c, h)
                spread = jnp.exp(jnp.minimum(col - rrow[c, pl.ds(h, 1), :], 0.0))
                scores = jnp.where(tri_r >= tri_c, mm(q, k, 1, 1) * spread, 0.0)
                s_hi, s_lo = split(scores)
                t_hi, t_lo = split(state)
                o = mm(s_hi, v) + mm(s_lo, v) + (mm(q, t_hi) + mm(q, t_lo)) * jnp.exp(col)
                scale = lax.rsqrt(jnp.mean(o * o, axis=1, keepdims=True) + 1e-06)
                osend[g, rows, qlanes] = (o * scale).astype(BF16)
                if c < CHUNKS - 1:
                    state = jnp.exp(ends[c, pl.ds(h, 1), :]) * state + ub[c, h]
            return inner

        lax.fori_loop(0, GH, head, 0)
        for i in range(PEERS):
            o_copy(g, i, block(to[i]), mine).start()
        ret[g, mine, :] = osend[g, mine, :]

    def stage(s, carry):
        def turn(r, step):
            g = s - 1 - r

            @pl.when(jnp.logical_and(g >= 0, g < GROUPS))
            def _():
                take_state(r, g)
                lax.fori_loop(g * GH, (g + 1) * GH, step, 0)
                if r < 2:
                    send_state(r + 1, g)
                else:
                    emit(g)

        turn(2, round2)

        @pl.when(s < GROUPS)
        def _():
            lax.fori_loop(s * GP, (s + 1) * GP, project, 0)
            send_state(0, s)

        @pl.when(s == 0)
        def _():
            for d in range(1, BACK + 1):

                @pl.when(tm >= d)
                def _():
                    a_copy(d).wait_recv()

        turn(1, round1)
        turn(0, round0)
        return carry

    lax.fori_loop(0, GROUPS + 3, stage, 0)


    def out_copy(g):
        cols = pl.ds(pl.multiple_of(g * GW, GW), GW)
        return pltpu.make_async_copy(outb.at[:, cols], out_hbm.at[:, cols], out_sem.at[g])

    def finish(g, carry):
        o_copy(g, 0, every, every).wait_recv()
        for half in range(GW // 256):
            cols = slice(half * 256, half * 256 + 256)
            where = pl.ds(pl.multiple_of(g * GW + half * 256, 256), 256)
            got = ret[g, :, cols]
            outb[:, where] = (mm(chi[...], got) + mm(clo[...], got)).astype(BF16)
        out_copy(g).start()
        return carry

    lax.fori_loop(0, GROUPS, finish, 0)

    whole(slotp, sps.at[0], spr.at[0]).wait_send()
    whole(xp, xps.at[0], xpr.at[0]).wait_send()
    whole(qp, qps.at[0], qpr.at[0]).wait_send()
    whole(recvd.at[0:PEERS], ds_.at[0], dr.at[0]).wait_send()
    for g in range(QUARTERS):
        whole(recvx.at[half_every, :QW], xs.at[g], xr.at[g]).wait_send()
    for j in range(PAIRS):
        whole(recvq.at[j, half_every], qs.at[j], qr.at[j]).wait_send()
    for g in range(GROUPS):
        o_copy(g, 0, every, every).wait_send()
        out_copy(g).wait()
    for r in range(3):

        @pl.when(tm + (1 << r) < TM)
        def _():
            whole(ssend.at[r], ss.at[r], sr.at[r, 0]).wait_send()

    for d in range(1, BACK + 1):

        @pl.when(tm + d < TM)
        def _():
            a_copy(d).wait_send()


def on_device(tokens, queries, log_decay, route_ids, gate_weights, kv_weight):
    anywhere = pl.BlockSpec(memory_space=pl.ANY)
    near = pl.BlockSpec(memory_space=pltpu.VMEM)
    dma = pltpu.SemaphoreType.DMA
    return pl.pallas_call(
        kernel,
        out_shape=jax.ShapeDtypeStruct((TOK, D), BF16),
        in_specs=[anywhere, anywhere, near, near, near, anywhere],
        out_specs=anywhere,
        scratch_shapes=[
            pltpu.VMEM((TOK, D), BF16),
            pltpu.VMEM((TOK, D), BF16),
            pltpu.VMEM((D, 2 * D), BF16),
            pltpu.VMEM((ROWS + 128, TOK), BF16),
            pltpu.VMEM((QUARTERS, 2, HALF * CAP, TOK), BF16),
            pltpu.VMEM((TOK, ROWS), BF16),
            pltpu.VMEM((TOK, ROWS), BF16),
            pltpu.VMEM((8, TOK), F32),
            pltpu.VMEM((QUARTERS, 8, TOK), F32),
            pltpu.VMEM((QUARTERS, TOK, QW), BF16),
            pltpu.VMEM((QUARTERS, 2, TOK, 256), BF16),
            pltpu.VMEM((MEMBERS, H, 128), BF16),
            pltpu.VMEM((MEMBERS, H, 128), BF16),
            pltpu.VMEM((QUARTERS, 2, HALF * CAP, QW), BF16),
            pltpu.VMEM((ROWS, D), BF16),
            pltpu.VMEM((PAIRS, 2, HALF * CAP, 256), BF16),
            pltpu.VMEM((PAIRS, ROWS, 256), BF16),
            pltpu.VMEM((PAIRS, ROWS, 256), BF16),
            pltpu.VMEM((PAIRS, ROWS, 256), BF16),
            pltpu.VMEM((GROUPS, ROWS, GW), BF16),
            pltpu.VMEM((GROUPS, ROWS, GW), BF16),
            pltpu.VMEM((TOK, D), BF16),
            pltpu.VMEM((CHUNKS, CHUNK, HD), F32),
            pltpu.VMEM((CHUNKS, H, CHUNK), F32),
            pltpu.VMEM((CHUNKS, H, HD), F32),
            pltpu.VMEM((H, HD), F32),
            pltpu.VMEM((BACK, H, HD), F32),
            pltpu.VMEM((CHUNKS - 1, H, HD, HD), F32),
            pltpu.VMEM((H, HD, HD), F32),
            pltpu.VMEM((H, HD, HD), F32),
            pltpu.VMEM((3, H, HD, HD), BF16),
            pltpu.VMEM((3, H, HD, HD), BF16),
            dma((3,)),
            dma((1,)),
            dma((QUARTERS,)),
            dma((1,)),
            dma((QUARTERS,)),
            dma((1,)),
            dma((QUARTERS,)),
            dma((1,)),
            dma((1,)),
            dma((QUARTERS,)),
            dma((QUARTERS,)),
            dma((PAIRS,)),
            dma((PAIRS,)),
            dma((GROUPS,)),
            dma((GROUPS,)),
            dma((BACK,)),
            dma((BACK,)),
            dma((3,)),
            dma((3, GROUPS)),
            dma((GROUPS,)),
        ],
        compiler_params=pltpu.CompilerParams(
            collective_id=0, has_side_effects=True, vmem_limit_bytes=60 * 2**20
        ),
        name="memories",
    )(tokens, queries, log_decay.T, route_ids.T, gate_weights.T, kv_weight)


def solution(mesh):
    rows = P(("tm", "mem"), None)
    return jax.shard_map(
        on_device,
        mesh=mesh,
        in_specs=(rows, rows, rows, rows, rows, P("mem", None, None)),
        out_specs=rows,
        check_vma=False,
    )
```

```python
import functools

import jax
import jax.numpy as jnp
from jax import lax
from jax.experimental import pallas as pl
from jax.experimental.pallas import tpu as pltpu
from jax.sharding import PartitionSpec as P

MESH = pl.DeviceIdType.MESH
F32, BF16 = jnp.float32, jnp.bfloat16

MEM_Y, MEM_Z = 4, 4
MEMBERS = MEM_Y * MEM_Z
TM = 8
TOK = 256
CAP = 48
ROWS = MEMBERS * CAP
D = 2048
H = 16
HD = 128
CHUNK = 256
CHUNKS = ROWS // CHUNK
GROUPS = 4
GW = D // GROUPS
GH = H // GROUPS
PAIRS = H // 2
GP = PAIRS // GROUPS

SHIFTS = (
    (2, 2), (0, 2), (2, 0), (3, 2), (1, 2),
    (2, 3), (2, 1), (3, 1), (1, 3), (3, 3),
    (3, 0), (0, 3), (0, 1), (1, 1), (1, 0),
)
PEERS = len(SHIFTS)
HALF_SHIFTS = ((1, 2), (0, 2), (1, 1), (1, 3), (0, 1), (0, 3), (1, 0))
HALF = MEMBERS // 2
HALF_PEERS = len(HALF_SHIFTS)
QUARTERS = 4
QW = D // QUARTERS
BACK = 3


def mm(a, b, da=1, db=0):
    return lax.dot_general(a, b, (((da,), (db,)), ((), ())), preferred_element_type=F32)


def split(a):
    high = a.astype(BF16)
    return high, (a - high.astype(F32)).astype(BF16)


def kernel(
    tok_hbm, qry_hbm, dec_ref, route_ref, gate_ref, w_hbm, out_hbm,
    tok, qry, w, onehot, picks, chi, clo, slots, slotp, xp, qp,
    sendd, recvd, sendx, recvx, sendq, recvq, kb, vb, osend, ret, outb,
    rcol, rrow, ends, atot, aprev, ub, inc, exc, ssend, srecv,
    load_sem, sps, spr, xps, xpr, qps, qpr, ds_, dr,
    xs, xr, qs, qr, os_, or_, as_, ar, ss, sr, out_sem,
):
    tm = lax.axis_index("tm")
    me = lax.axis_index("mem")
    my, mz = lax.div(me, MEM_Z), lax.rem(me, MEM_Z)

    def at(dy, dz):
        return lax.rem(my + dy, MEM_Y) * MEM_Z + lax.rem(mz + dz, MEM_Z)

    core = lax.rem(tm, 2)
    turned = [(dy + core * (dz - dy), dz + core * (dy - dz)) for dy, dz in SHIFTS]
    to = [at(dy, dz) for dy, dz in turned]

    y_swap, y_flip = my + 1 - 2 * lax.rem(my, 2), MEM_Y - 1 - my
    z_swap, z_flip = mz + 1 - 2 * lax.rem(mz, 2), MEM_Z - 1 - mz
    partner = (
        y_swap * MEM_Z + mz,
        y_flip * MEM_Z + mz,
        my * MEM_Z + z_swap,
        my * MEM_Z + z_flip,
    )
    other = (y_flip, y_swap, z_flip, z_swap)

    def in_half(g, across, step):
        if g < 2:
            ring = lax.rem(mz + step, MEM_Z)
            return (other[g] if across else my) * MEM_Z + ring, across * 4 + ring
        ring = lax.rem(my + step, MEM_Y)
        return ring * MEM_Z + (other[g] if across else mz), across * 4 + ring

    def in_turn(g, across, step):
        swap = (g + 2) % QUARTERS
        (place, number), (place2, number2) = in_half(g, across, step), in_half(swap, across, step)
        return (
            g + core * (swap - g),
            place + core * (place2 - place),
            number + core * (number2 - number),
            partner[g] + core * (partner[swap] - partner[g]),
        )

    def block(place):
        return pl.ds(pl.multiple_of(place * CAP, 16), CAP)

    load_tok = pltpu.make_async_copy(tok_hbm, tok, load_sem.at[0])
    load_qry = pltpu.make_async_copy(qry_hbm, qry, load_sem.at[1])
    load_w = pltpu.make_async_copy(w_hbm.at[0], w, load_sem.at[2])
    load_tok.start()
    load_qry.start()

    barrier = pltpu.get_barrier_semaphore()
    for i in range(PEERS):
        pl.semaphore_signal(barrier, inc=1, device_id=(tm, to[i]), device_id_type=MESH)
    for d in range(1, TM):
        pl.semaphore_signal(
            barrier, inc=1, device_id=(lax.rem(tm + d, TM), me), device_id_type=MESH
        )

    r0, r1 = route_ref[0:1, :], route_ref[1:2, :]
    mem_row = lax.broadcasted_iota(jnp.int32, (MEMBERS, TOK), 0)
    hot0 = (mem_row == r0).astype(F32)
    hot1 = (mem_row == r1).astype(F32)
    ahead = (
        lax.broadcasted_iota(jnp.int32, (TOK, TOK), 0)
        < lax.broadcasted_iota(jnp.int32, (TOK, TOK), 1)
    ).astype(BF16)
    rank = mm((hot0 + hot1).astype(BF16), ahead)
    slot0 = r0.astype(F32) * CAP + jnp.sum(hot0 * rank, axis=0, keepdims=True)
    slot1 = r1.astype(F32) * CAP + jnp.sum(hot1 * rank, axis=0, keepdims=True)
    slots[...] = jnp.concatenate([slot0, slot1, jnp.zeros((6, TOK), F32)], axis=0)
    slot_row = lax.broadcasted_iota(jnp.int32, (ROWS + 128, TOK), 0).astype(F32)
    is0, is1 = slot_row == slot0, slot_row == slot1
    onehot[...] = (is0.astype(F32) + is1.astype(F32)).astype(BF16)

    def gather_d(e, c):
        rows = onehot[pl.ds(pl.multiple_of(e * CAP, 16), 128), :]
        sendd[e] = mm(dec_ref[...], rows, 1, 1).astype(BF16)
        return c

    def slot_copy(g):
        return pltpu.make_async_remote_copy(
            src_ref=slots,
            dst_ref=slotp.at[g],
            send_sem=sps.at[0],
            recv_sem=spr.at[g],
            device_id=(tm, partner[g]),
            device_id_type=MESH,
        )

    def xp_copy(g):
        return pltpu.make_async_remote_copy(
            src_ref=tok_hbm.at[:, g * QW : (g + 1) * QW],
            dst_ref=xp.at[g],
            send_sem=xps.at[0],
            recv_sem=xpr.at[g],
            device_id=(tm, partner[g]),
            device_id_type=MESH,
        )

    def qp_copy(g, u):
        first = (u * QUARTERS + g) * 256
        return pltpu.make_async_remote_copy(
            src_ref=qry_hbm.at[:, first : first + 256],
            dst_ref=qp.at[g, u],
            send_sem=qps.at[0],
            recv_sem=qpr.at[g],
            device_id=(tm, partner[g]),
            device_id_type=MESH,
        )

    def whole(ref, send_sem, recv_sem):
        return pltpu.make_async_remote_copy(
            src_ref=ref,
            dst_ref=ref,
            send_sem=send_sem,
            recv_sem=recv_sem,
            device_id=(tm, to[0]),
            device_id_type=MESH,
        )

    def d_copy(i):
        return pltpu.make_async_remote_copy(
            src_ref=sendd.at[to[i]],
            dst_ref=recvd.at[me],
            send_sem=ds_.at[0],
            recv_sem=dr.at[0],
            device_id=(tm, to[i]),
            device_id_type=MESH,
        )

    def x_copy(g, own, src, dst, place):
        return pltpu.make_async_remote_copy(
            src_ref=sendx.at[g, own, src],
            dst_ref=recvx.at[dst, pl.ds(pl.multiple_of(g * QW, QW), QW)],
            send_sem=xs.at[g],
            recv_sem=xr.at[g],
            device_id=(tm, place),
            device_id_type=MESH,
        )

    def q_copy(j, own, src, dst, place):
        return pltpu.make_async_remote_copy(
            src_ref=sendq.at[j, own, src],
            dst_ref=recvq.at[j, dst],
            send_sem=qs.at[j],
            recv_sem=qr.at[j],
            device_id=(tm, place),
            device_id_type=MESH,
        )

    def o_copy(g, i, src, dst):
        return pltpu.make_async_remote_copy(
            src_ref=osend.at[g, src],
            dst_ref=ret.at[g, dst],
            send_sem=os_.at[g],
            recv_sem=or_.at[g],
            device_id=(tm, to[i]),
            device_id_type=MESH,
        )

    every = slice(0, PEERS * CAP)
    half_every = slice(0, 2 * HALF_PEERS * CAP)

    def a_copy(d):
        return pltpu.make_async_remote_copy(
            src_ref=atot,
            dst_ref=aprev.at[d - 1],
            send_sem=as_.at[d - 1],
            recv_sem=ar.at[d - 1],
            device_id=(lax.rem(tm + d, TM), me),
            device_id_type=MESH,
        )

    def s_copy(r, g):
        heads = pl.ds(g * GH, GH)
        return pltpu.make_async_remote_copy(
            src_ref=ssend.at[r, heads],
            dst_ref=srecv.at[r, heads],
            send_sem=ss.at[r],
            recv_sem=sr.at[r, g],
            device_id=(lax.rem(tm + (1 << r), TM), me),
            device_id_type=MESH,
        )

    pl.semaphore_wait(barrier, PEERS + TM - 1)
    for g in range(QUARTERS):
        slot_copy(g).start()
    for g in range(QUARTERS):
        xp_copy(g).start()
    lax.fori_loop(0, MEMBERS, gather_d, 0)
    for i in range(PEERS):
        d_copy(i).start()
    for u in range(2):
        for g in range(QUARTERS):
            qp_copy(g, u).start()
    recvd[me] = sendd[me]

    pick_row = lax.broadcasted_iota(jnp.int32, (HALF * CAP, TOK), 0)
    over = (pick_row >= HALF * CAP // 2).astype(jnp.int32)
    ring_row = pick_row - over * (HALF * CAP // 2)
    ring = sum((ring_row >= k * CAP).astype(jnp.int32) for k in range(1, 4))

    def wanted(g):
        if g < 2:
            return (ring_row + (my + over * (other[g] - my)) * (MEM_Z * CAP)).astype(F32)
        column_slot = (mz + over * (other[g] - mz)) * CAP
        return (ring_row + ring * ((MEM_Z - 1) * CAP) + column_slot).astype(F32)

    def pick(g, slots_now):
        goal = wanted(g)
        first, second = goal == slots_now[0:1, :], goal == slots_now[1:2, :]
        return (first.astype(F32) + second.astype(F32)).astype(BF16)

    load_tok.wait()
    for g in range(QUARTERS):
        picks[g, 0] = pick(g, slots[...])
        sendx[g, 0] = mm(picks[g, 0], tok[:, g * QW : (g + 1) * QW]).astype(BF16)
    for g in range(QUARTERS):
        slot_copy(g).wait_recv()
        picks[g, 1] = pick(g, slotp[g])
    for g in range(QUARTERS):
        whole(xp.at[g], xps.at[0], xpr.at[g]).wait_recv()
        sendx[g, 1] = mm(picks[g, 1], xp[g]).astype(BF16)
    mine = block(me)
    for across, step in HALF_SHIFTS:
        for g in range(QUARTERS):
            quarter, place, number, mate = in_turn(g, across, step)
            for own in range(2):
                dst = block(mate) if own else mine
                x_copy(quarter, own, block(number), dst, place).start()
    load_w.start()
    for g in range(QUARTERS):
        number = in_half(g, 0, 0)[1]
        cols = slice(g * QW, (g + 1) * QW)
        recvx[mine, cols] = sendx[g, 0, block(number), :]
        recvx[block(partner[g]), cols] = sendx[g, 1, block(number), :]

    load_qry.wait()
    for g in range(QUARTERS):
        whole(qp.at[g], qps.at[0], qpr.at[g]).wait_recv()

    def gather_q(u, c):
        for g in range(QUARTERS):
            j = u * QUARTERS + g
            cols = pl.ds(pl.multiple_of(j * 256, 256), 256)
            sendq[j, 0] = mm(picks[g, 0], qry[:, cols]).astype(BF16)
            sendq[j, 1] = mm(picks[g, 1], qp[g, u]).astype(BF16)
        for across, step in HALF_SHIFTS:
            for g in range(QUARTERS):
                quarter, place, number, mate = in_turn(g, across, step)
                j = u * QUARTERS + quarter
                for own in range(2):
                    dst = block(mate) if own else mine
                    q_copy(j, own, block(number), dst, place).start()
        for g in range(QUARTERS):
            j = u * QUARTERS + g
            number = in_half(g, 0, 0)[1]
            recvq[j, mine, :] = sendq[j, 0, block(number), :]
            recvq[j, block(partner[g]), :] = sendq[j, 1, block(number), :]
        return c

    lax.fori_loop(0, 2, gather_q, 0)

    for r in range(3):

        @pl.when(tm < (1 << r))
        def _():
            srecv[r] = jnp.zeros((H, HD, HD), BF16)

    for d in range(1, BACK + 1):

        @pl.when(tm < d)
        def _():
            aprev[d - 1] = jnp.zeros((H, HD), F32)

    gates = jnp.where(is0, gate_ref[0:1, :], 0.0) + jnp.where(is1, gate_ref[1:2, :], 0.0)
    gates = gates[:ROWS]
    gates_hi, gates_lo = split(gates)
    chi[...] = gates_hi.T
    clo[...] = gates_lo.T

    whole(recvd.at[0:PEERS], ds_.at[0], dr.at[0]).wait_recv()
    tri_r = lax.broadcasted_iota(jnp.int32, (CHUNK, CHUNK), 0)
    tri_c = lax.broadcasted_iota(jnp.int32, (CHUNK, CHUNK), 1)
    place_row = lax.broadcasted_iota(jnp.int32, (128, CHUNK), 0)
    place_col = lax.broadcasted_iota(jnp.int32, (128, CHUNK), 1)
    used = place_row < CAP

    def add_logs(src, sums):
        at_row = place_row + src * CAP
        out = []
        for c in range(CHUNKS):
            within = jnp.logical_and(at_row >= c * CHUNK, at_row <= place_col + c * CHUNK)
            take = jnp.where(jnp.logical_and(used, within), 1.0, 0.0).astype(BF16)
            out.append(sums[c] + mm(recvd[src], take))
        return tuple(out)

    sums = lax.fori_loop(
        0, MEMBERS, add_logs, tuple(jnp.zeros((H, CHUNK), F32) for c in range(CHUNKS))
    )
    total = jnp.zeros((H, HD), F32)
    for c in range(CHUNKS):
        rows = sums[c]
        rrow[c] = rows
        rcol[c] = jnp.concatenate([rows, jnp.zeros((HD - H, CHUNK), F32)], axis=0).T
        end = jnp.broadcast_to(rows[:, CHUNK - 1 : CHUNK], (H, HD))
        ends[c] = end
        total = total + end
    atot[...] = total
    for d in range(1, BACK + 1):

        @pl.when(tm + d < TM)
        def _():
            a_copy(d).start()

    load_w.wait()
    for g in range(QUARTERS):
        x_copy(g, 0, slice(0, CAP), half_every, to[0]).wait_recv()

    lane = lax.broadcasted_iota(jnp.int32, (CHUNK, HD), 1)

    def column(c, h):
        return jnp.sum(jnp.where(lane == h, rcol[c], 0.0), axis=1, keepdims=True)

    def project(j, carry):
        def columns(first):
            cols = pl.ds(pl.multiple_of(first, 256), 256)
            return mm(recvx[...], w[:, cols]).astype(BF16)

        kb[j] = columns(j * 256)
        vb[j] = columns(D + j * 256)
        for hh in range(2):
            h = 2 * j + hh
            lanes = slice(hh * HD, hh * HD + HD)
            local = None
            for c in range(CHUNKS):
                rows = slice(c * CHUNK, (c + 1) * CHUNK)
                end = ends[c, pl.ds(h, 1), :]
                fade = jnp.exp(end - column(c, h))
                keys = (kb[j, rows, lanes].astype(F32) * fade).astype(BF16)
                part = mm(keys, vb[j, rows, lanes], 0, 0)
                if c < CHUNKS - 1:
                    ub[c, h] = part
                local = part if c == 0 else jnp.exp(end) * local + part
            inc[h] = local
            ssend[0, h] = local.astype(BF16)
        return carry

    def gain(h, first, last):
        span = aprev[first, pl.ds(h, 1), :]
        for d in range(first + 1, last):
            span = span + aprev[d, pl.ds(h, 1), :]
        return span

    def round0(h, carry):
        got = srecv[0, h].astype(F32)
        exc[h] = got
        new = jnp.exp(atot[pl.ds(h, 1), :]) * got + inc[h]
        inc[h] = new
        ssend[1, h] = new.astype(BF16)
        return carry

    def round1(h, carry):
        got = srecv[1, h].astype(F32)
        before = gain(h, 0, 1)
        exc[h] = jnp.exp(before) * got + exc[h]
        new = jnp.exp(before + atot[pl.ds(h, 1), :]) * got + inc[h]
        ssend[2, h] = new.astype(BF16)
        return carry

    def round2(h, carry):
        got = srecv[2, h].astype(F32)
        exc[h] = jnp.exp(gain(h, 0, 3)) * got + exc[h]
        return carry

    def send_state(r, g):
        @pl.when(tm + (1 << r) < TM)
        def _():
            s_copy(r, g).start()

    def take_state(r, g):
        @pl.when(tm >= (1 << r))
        def _():
            s_copy(r, g).wait_recv()

    def emit(g):
        for p in range(2):
            q_copy(2 * g + p, 0, slice(0, CAP), half_every, to[0]).wait_recv()

        def head(hh, inner):
            h = g * GH + hh
            j = lax.div(h, 2)
            klanes = pl.ds(pl.multiple_of(lax.rem(h, 2) * HD, HD), HD)
            qlanes = pl.ds(pl.multiple_of(hh * HD, HD), HD)
            state = exc[h]
            for c in range(CHUNKS):
                rows = slice(c * CHUNK, (c + 1) * CHUNK)
                q = recvq[j, rows, klanes]
                k = kb[j, rows, klanes]
                v = vb[j, rows, klanes]
                col = column(c, h)
                spread = jnp.exp(jnp.minimum(col - rrow[c, pl.ds(h, 1), :], 0.0))
                scores = jnp.where(tri_r >= tri_c, mm(q, k, 1, 1) * spread, 0.0)
                s_hi, s_lo = split(scores)
                t_hi, t_lo = split(state)
                o = mm(s_hi, v) + mm(s_lo, v) + (mm(q, t_hi) + mm(q, t_lo)) * jnp.exp(col)
                scale = lax.rsqrt(jnp.mean(o * o, axis=1, keepdims=True) + 1e-06)
                osend[g, rows, qlanes] = (o * scale).astype(BF16)
                if c < CHUNKS - 1:
                    state = jnp.exp(ends[c, pl.ds(h, 1), :]) * state + ub[c, h]
            return inner

        lax.fori_loop(0, GH, head, 0)
        for i in range(PEERS):
            o_copy(g, i, block(to[i]), mine).start()
        ret[g, mine, :] = osend[g, mine, :]

    def stage(s, carry):
        def turn(r, step):
            g = s - 1 - r

            @pl.when(jnp.logical_and(g >= 0, g < GROUPS))
            def _():
                take_state(r, g)
                lax.fori_loop(g * GH, (g + 1) * GH, step, 0)
                if r < 2:
                    send_state(r + 1, g)
                else:
                    emit(g)

        turn(2, round2)

        @pl.when(s < GROUPS)
        def _():
            lax.fori_loop(s * GP, (s + 1) * GP, project, 0)
            send_state(0, s)

        @pl.when(s == 0)
        def _():
            for d in range(1, BACK + 1):

                @pl.when(tm >= d)
                def _():
                    a_copy(d).wait_recv()

        turn(1, round1)
        turn(0, round0)
        return carry

    lax.fori_loop(0, GROUPS + 3, stage, 0)


    def out_copy(g):
        cols = pl.ds(pl.multiple_of(g * GW, GW), GW)
        return pltpu.make_async_copy(outb.at[:, cols], out_hbm.at[:, cols], out_sem.at[g])

    def finish(g, carry):
        o_copy(g, 0, every, every).wait_recv()
        for half in range(GW // 256):
            cols = slice(half * 256, half * 256 + 256)
            where = pl.ds(pl.multiple_of(g * GW + half * 256, 256), 256)
            got = ret[g, :, cols]
            outb[:, where] = (mm(chi[...], got) + mm(clo[...], got)).astype(BF16)
        out_copy(g).start()
        return carry

    lax.fori_loop(0, GROUPS, finish, 0)

    whole(slotp, sps.at[0], spr.at[0]).wait_send()
    whole(xp, xps.at[0], xpr.at[0]).wait_send()
    whole(qp, qps.at[0], qpr.at[0]).wait_send()
    whole(recvd.at[0:PEERS], ds_.at[0], dr.at[0]).wait_send()
    for g in range(QUARTERS):
        whole(recvx.at[half_every, :QW], xs.at[g], xr.at[g]).wait_send()
    for j in range(PAIRS):
        whole(recvq.at[j, half_every], qs.at[j], qr.at[j]).wait_send()
    for g in range(GROUPS):
        o_copy(g, 0, every, every).wait_send()
        out_copy(g).wait()
    for r in range(3):

        @pl.when(tm + (1 << r) < TM)
        def _():
            whole(ssend.at[r], ss.at[r], sr.at[r, 0]).wait_send()

    for d in range(1, BACK + 1):

        @pl.when(tm + d < TM)
        def _():
            a_copy(d).wait_send()


def on_device(tokens, queries, log_decay, route_ids, gate_weights, kv_weight):
    anywhere = pl.BlockSpec(memory_space=pl.ANY)
    near = pl.BlockSpec(memory_space=pltpu.VMEM)
    dma = pltpu.SemaphoreType.DMA
    return pl.pallas_call(
        kernel,
        out_shape=jax.ShapeDtypeStruct((TOK, D), BF16),
        in_specs=[anywhere, anywhere, near, near, near, anywhere],
        out_specs=anywhere,
        scratch_shapes=[
            pltpu.VMEM((TOK, D), BF16),
            pltpu.VMEM((TOK, D), BF16),
            pltpu.VMEM((D, 2 * D), BF16),
            pltpu.VMEM((ROWS + 128, TOK), BF16),
            pltpu.VMEM((QUARTERS, 2, HALF * CAP, TOK), BF16),
            pltpu.VMEM((TOK, ROWS), BF16),
            pltpu.VMEM((TOK, ROWS), BF16),
            pltpu.VMEM((8, TOK), F32),
            pltpu.VMEM((QUARTERS, 8, TOK), F32),
            pltpu.VMEM((QUARTERS, TOK, QW), BF16),
            pltpu.VMEM((QUARTERS, 2, TOK, 256), BF16),
            pltpu.VMEM((MEMBERS, H, 128), BF16),
            pltpu.VMEM((MEMBERS, H, 128), BF16),
            pltpu.VMEM((QUARTERS, 2, HALF * CAP, QW), BF16),
            pltpu.VMEM((ROWS, D), BF16),
            pltpu.VMEM((PAIRS, 2, HALF * CAP, 256), BF16),
            pltpu.VMEM((PAIRS, ROWS, 256), BF16),
            pltpu.VMEM((PAIRS, ROWS, 256), BF16),
            pltpu.VMEM((PAIRS, ROWS, 256), BF16),
            pltpu.VMEM((GROUPS, ROWS, GW), BF16),
            pltpu.VMEM((GROUPS, ROWS, GW), BF16),
            pltpu.VMEM((TOK, D), BF16),
            pltpu.VMEM((CHUNKS, CHUNK, HD), F32),
            pltpu.VMEM((CHUNKS, H, CHUNK), F32),
            pltpu.VMEM((CHUNKS, H, HD), F32),
            pltpu.VMEM((H, HD), F32),
            pltpu.VMEM((BACK, H, HD), F32),
            pltpu.VMEM((CHUNKS - 1, H, HD, HD), F32),
            pltpu.VMEM((H, HD, HD), F32),
            pltpu.VMEM((H, HD, HD), F32),
            pltpu.VMEM((3, H, HD, HD), BF16),
            pltpu.VMEM((3, H, HD, HD), BF16),
            dma((3,)),
            dma((1,)),
            dma((QUARTERS,)),
            dma((1,)),
            dma((QUARTERS,)),
            dma((1,)),
            dma((QUARTERS,)),
            dma((1,)),
            dma((1,)),
            dma((QUARTERS,)),
            dma((QUARTERS,)),
            dma((PAIRS,)),
            dma((PAIRS,)),
            dma((GROUPS,)),
            dma((GROUPS,)),
            dma((BACK,)),
            dma((BACK,)),
            dma((3,)),
            dma((3, GROUPS)),
            dma((GROUPS,)),
        ],
        compiler_params=pltpu.CompilerParams(
            collective_id=0, has_side_effects=True, vmem_limit_bytes=60 * 2**20
        ),
        name="memories",
    )(tokens, queries, log_decay.T, route_ids.T, gate_weights.T, kv_weight)


def solution(mesh):
    rows = P(("tm", "mem"), None)
    return jax.shard_map(
        on_device,
        mesh=mesh,
        in_specs=(rows, rows, rows, rows, rows, P("mem", None, None)),
        out_specs=rows,
        check_vma=False,
    )
```

```python
import functools

import jax
import jax.numpy as jnp
from jax import lax
from jax.experimental import pallas as pl
from jax.experimental.pallas import tpu as pltpu
from jax.sharding import PartitionSpec as P

MESH = pl.DeviceIdType.MESH
F32, BF16 = jnp.float32, jnp.bfloat16

MEM_Y, MEM_Z = 4, 4
MEMBERS = MEM_Y * MEM_Z
TM = 8
TOK = 256
CAP = 48
ROWS = MEMBERS * CAP
D = 2048
H = 16
HD = 128
CHUNK = 256
CHUNKS = ROWS // CHUNK
GROUPS = 4
GW = D // GROUPS
GH = H // GROUPS
PAIRS = H // 2
GP = PAIRS // GROUPS

SHIFTS = (
    (2, 2), (0, 2), (2, 0), (3, 2), (1, 2),
    (2, 3), (2, 1), (3, 1), (1, 3), (3, 3),
    (3, 0), (0, 3), (0, 1), (1, 1), (1, 0),
)
PEERS = len(SHIFTS)
HALF_SHIFTS = ((1, 2), (0, 2), (1, 1), (1, 3), (0, 1), (0, 3), (1, 0))
HALF = MEMBERS // 2
HALF_PEERS = len(HALF_SHIFTS)
QUARTERS = 4
QW = D // QUARTERS
BACK = 3


def mm(a, b, da=1, db=0):
    return lax.dot_general(a, b, (((da,), (db,)), ((), ())), preferred_element_type=F32)


def split(a):
    high = a.astype(BF16)
    return high, (a - high.astype(F32)).astype(BF16)


def kernel(
    tok_hbm, qry_hbm, dec_ref, route_ref, gate_ref, w_hbm, out_hbm,
    tok, qry, w, onehot, picks, chi, clo, slots, slotp, xp, qp,
    sendd, recvd, sendx, recvx, sendq, recvq, kb, vb, osend, ret, outb,
    rcol, rrow, ends, atot, aprev, ub, inc, exc, ssend, srecv,
    load_sem, sps, spr, xps, xpr, qps, qpr, ds_, dr,
    xs, xr, qs, qr, os_, or_, as_, ar, ss, sr, out_sem,
):
    tm = lax.axis_index("tm")
    me = lax.axis_index("mem")
    my, mz = lax.div(me, MEM_Z), lax.rem(me, MEM_Z)

    def at(dy, dz):
        return lax.rem(my + dy, MEM_Y) * MEM_Z + lax.rem(mz + dz, MEM_Z)

    core = lax.rem(tm, 2)
    turned = [(dy + core * (dz - dy), dz + core * (dy - dz)) for dy, dz in SHIFTS]
    to = [at(dy, dz) for dy, dz in turned]

    y_swap, y_flip = my + 1 - 2 * lax.rem(my, 2), MEM_Y - 1 - my
    z_swap, z_flip = mz + 1 - 2 * lax.rem(mz, 2), MEM_Z - 1 - mz
    partner = (
        y_swap * MEM_Z + mz,
        y_flip * MEM_Z + mz,
        my * MEM_Z + z_swap,
        my * MEM_Z + z_flip,
    )
    other = (y_flip, y_swap, z_flip, z_swap)

    def in_half(g, across, step):
        if g < 2:
            ring = lax.rem(mz + step, MEM_Z)
            return (other[g] if across else my) * MEM_Z + ring, across * 4 + ring
        ring = lax.rem(my + step, MEM_Y)
        return ring * MEM_Z + (other[g] if across else mz), across * 4 + ring

    def in_turn(g, across, step):
        swap = (g + 2) % QUARTERS
        (place, number), (place2, number2) = in_half(g, across, step), in_half(swap, across, step)
        return (
            g + core * (swap - g),
            place + core * (place2 - place),
            number + core * (number2 - number),
            partner[g] + core * (partner[swap] - partner[g]),
        )

    def block(place):
        return pl.ds(pl.multiple_of(place * CAP, 16), CAP)

    load_tok = pltpu.make_async_copy(tok_hbm, tok, load_sem.at[0])
    load_qry = pltpu.make_async_copy(qry_hbm, qry, load_sem.at[1])
    load_w = pltpu.make_async_copy(w_hbm.at[0], w, load_sem.at[2])
    load_tok.start()
    load_qry.start()

    barrier = pltpu.get_barrier_semaphore()
    for i in range(PEERS):
        pl.semaphore_signal(barrier, inc=1, device_id=(tm, to[i]), device_id_type=MESH)
    for d in range(1, TM):
        pl.semaphore_signal(
            barrier, inc=1, device_id=(lax.rem(tm + d, TM), me), device_id_type=MESH
        )

    r0, r1 = route_ref[0:1, :], route_ref[1:2, :]
    mem_row = lax.broadcasted_iota(jnp.int32, (MEMBERS, TOK), 0)
    hot0 = (mem_row == r0).astype(F32)
    hot1 = (mem_row == r1).astype(F32)
    ahead = (
        lax.broadcasted_iota(jnp.int32, (TOK, TOK), 0)
        < lax.broadcasted_iota(jnp.int32, (TOK, TOK), 1)
    ).astype(BF16)
    rank = mm((hot0 + hot1).astype(BF16), ahead)
    slot0 = r0.astype(F32) * CAP + jnp.sum(hot0 * rank, axis=0, keepdims=True)
    slot1 = r1.astype(F32) * CAP + jnp.sum(hot1 * rank, axis=0, keepdims=True)
    slots[...] = jnp.concatenate([slot0, slot1, jnp.zeros((6, TOK), F32)], axis=0)
    slot_row = lax.broadcasted_iota(jnp.int32, (ROWS + 128, TOK), 0).astype(F32)
    is0, is1 = slot_row == slot0, slot_row == slot1
    onehot[...] = (is0.astype(F32) + is1.astype(F32)).astype(BF16)

    def gather_d(e, c):
        rows = onehot[pl.ds(pl.multiple_of(e * CAP, 16), 128), :]
        sendd[e] = mm(dec_ref[...], rows, 1, 1).astype(BF16)
        return c

    def slot_copy(g):
        return pltpu.make_async_remote_copy(
            src_ref=slots,
            dst_ref=slotp.at[g],
            send_sem=sps.at[0],
            recv_sem=spr.at[g],
            device_id=(tm, partner[g]),
            device_id_type=MESH,
        )

    def xp_copy(g):
        return pltpu.make_async_remote_copy(
            src_ref=tok_hbm.at[:, g * QW : (g + 1) * QW],
            dst_ref=xp.at[g],
            send_sem=xps.at[0],
            recv_sem=xpr.at[g],
            device_id=(tm, partner[g]),
            device_id_type=MESH,
        )

    def qp_copy(g, u):
        first = (u * QUARTERS + g) * 256
        return pltpu.make_async_remote_copy(
            src_ref=qry_hbm.at[:, first : first + 256],
            dst_ref=qp.at[g, u],
            send_sem=qps.at[0],
            recv_sem=qpr.at[g],
            device_id=(tm, partner[g]),
            device_id_type=MESH,
        )

    def whole(ref, send_sem, recv_sem):
        return pltpu.make_async_remote_copy(
            src_ref=ref,
            dst_ref=ref,
            send_sem=send_sem,
            recv_sem=recv_sem,
            device_id=(tm, to[0]),
            device_id_type=MESH,
        )

    def d_copy(i):
        return pltpu.make_async_remote_copy(
            src_ref=sendd.at[to[i]],
            dst_ref=recvd.at[me],
            send_sem=ds_.at[0],
            recv_sem=dr.at[0],
            device_id=(tm, to[i]),
            device_id_type=MESH,
        )

    def x_copy(g, own, src, dst, place):
        return pltpu.make_async_remote_copy(
            src_ref=sendx.at[g, own, src],
            dst_ref=recvx.at[dst, pl.ds(pl.multiple_of(g * QW, QW), QW)],
            send_sem=xs.at[0],
            recv_sem=xr.at[0],
            device_id=(tm, place),
            device_id_type=MESH,
        )

    def q_copy(j, own, src, dst, place):
        return pltpu.make_async_remote_copy(
            src_ref=sendq.at[j, own, src],
            dst_ref=recvq.at[j, dst],
            send_sem=qs.at[0],
            recv_sem=qr.at[j],
            device_id=(tm, place),
            device_id_type=MESH,
        )

    def o_copy(g, i, src, dst):
        return pltpu.make_async_remote_copy(
            src_ref=osend.at[g, src],
            dst_ref=ret.at[g, dst],
            send_sem=os_.at[0],
            recv_sem=or_.at[g],
            device_id=(tm, to[i]),
            device_id_type=MESH,
        )

    every = slice(0, PEERS * CAP)
    half_every = slice(0, 2 * HALF_PEERS * CAP)

    def a_copy(d):
        return pltpu.make_async_remote_copy(
            src_ref=atot,
            dst_ref=aprev.at[d - 1],
            send_sem=as_.at[d - 1],
            recv_sem=ar.at[d - 1],
            device_id=(lax.rem(tm + d, TM), me),
            device_id_type=MESH,
        )

    def s_copy(r, g):
        heads = pl.ds(g * GH, GH)
        return pltpu.make_async_remote_copy(
            src_ref=ssend.at[r, heads],
            dst_ref=srecv.at[r, heads],
            send_sem=ss.at[r],
            recv_sem=sr.at[r, g],
            device_id=(lax.rem(tm + (1 << r), TM), me),
            device_id_type=MESH,
        )

    pl.semaphore_wait(barrier, PEERS + TM - 1)
    for g in range(QUARTERS):
        slot_copy(g).start()
    for g in range(QUARTERS):
        xp_copy(g).start()
    lax.fori_loop(0, MEMBERS, gather_d, 0)
    for i in range(PEERS):
        d_copy(i).start()
    for u in range(2):
        for g in range(QUARTERS):
            qp_copy(g, u).start()
    recvd[me] = sendd[me]

    pick_row = lax.broadcasted_iota(jnp.int32, (HALF * CAP, TOK), 0)
    over = (pick_row >= HALF * CAP // 2).astype(jnp.int32)
    ring_row = pick_row - over * (HALF * CAP // 2)
    ring = sum((ring_row >= k * CAP).astype(jnp.int32) for k in range(1, 4))

    def wanted(g):
        if g < 2:
            return (ring_row + (my + over * (other[g] - my)) * (MEM_Z * CAP)).astype(F32)
        column_slot = (mz + over * (other[g] - mz)) * CAP
        return (ring_row + ring * ((MEM_Z - 1) * CAP) + column_slot).astype(F32)

    def pick(g, slots_now):
        goal = wanted(g)
        first, second = goal == slots_now[0:1, :], goal == slots_now[1:2, :]
        return (first.astype(F32) + second.astype(F32)).astype(BF16)

    load_tok.wait()
    for g in range(QUARTERS):
        picks[g, 0] = pick(g, slots[...])
        sendx[g, 0] = mm(picks[g, 0], tok[:, g * QW : (g + 1) * QW]).astype(BF16)
    for g in range(QUARTERS):
        slot_copy(g).wait_recv()
        picks[g, 1] = pick(g, slotp[g])
    for g in range(QUARTERS):
        whole(xp.at[g], xps.at[0], xpr.at[g]).wait_recv()
        sendx[g, 1] = mm(picks[g, 1], xp[g]).astype(BF16)
    mine = block(me)
    for across, step in HALF_SHIFTS:
        for g in range(QUARTERS):
            quarter, place, number, mate = in_turn(g, across, step)
            for own in range(2):
                dst = block(mate) if own else mine
                x_copy(quarter, own, block(number), dst, place).start()
    load_w.start()
    for g in range(QUARTERS):
        number = in_half(g, 0, 0)[1]
        cols = slice(g * QW, (g + 1) * QW)
        recvx[mine, cols] = sendx[g, 0, block(number), :]
        recvx[block(partner[g]), cols] = sendx[g, 1, block(number), :]

    load_qry.wait()
    for g in range(QUARTERS):
        whole(qp.at[g], qps.at[0], qpr.at[g]).wait_recv()

    def gather_q(u, c):
        for g in range(QUARTERS):
            j = u * QUARTERS + g
            cols = pl.ds(pl.multiple_of(j * 256, 256), 256)
            sendq[j, 0] = mm(picks[g, 0], qry[:, cols]).astype(BF16)
            sendq[j, 1] = mm(picks[g, 1], qp[g, u]).astype(BF16)
        for across, step in HALF_SHIFTS:
            for g in range(QUARTERS):
                quarter, place, number, mate = in_turn(g, across, step)
                j = u * QUARTERS + quarter
                for own in range(2):
                    dst = block(mate) if own else mine
                    q_copy(j, own, block(number), dst, place).start()
        for g in range(QUARTERS):
            j = u * QUARTERS + g
            number = in_half(g, 0, 0)[1]
            recvq[j, mine, :] = sendq[j, 0, block(number), :]
            recvq[j, block(partner[g]), :] = sendq[j, 1, block(number), :]
        return c

    lax.fori_loop(0, 2, gather_q, 0)

    for r in range(3):

        @pl.when(tm < (1 << r))
        def _():
            srecv[r] = jnp.zeros((H, HD, HD), BF16)

    for d in range(1, BACK + 1):

        @pl.when(tm < d)
        def _():
            aprev[d - 1] = jnp.zeros((H, HD), F32)

    gates = jnp.where(is0, gate_ref[0:1, :], 0.0) + jnp.where(is1, gate_ref[1:2, :], 0.0)
    gates = gates[:ROWS]
    gates_hi, gates_lo = split(gates)
    chi[...] = gates_hi.T
    clo[...] = gates_lo.T

    whole(recvd.at[0:PEERS], ds_.at[0], dr.at[0]).wait_recv()
    tri_r = lax.broadcasted_iota(jnp.int32, (CHUNK, CHUNK), 0)
    tri_c = lax.broadcasted_iota(jnp.int32, (CHUNK, CHUNK), 1)
    place_row = lax.broadcasted_iota(jnp.int32, (128, CHUNK), 0)
    place_col = lax.broadcasted_iota(jnp.int32, (128, CHUNK), 1)
    used = place_row < CAP

    def add_logs(src, sums):
        at_row = place_row + src * CAP
        out = []
        for c in range(CHUNKS):
            within = jnp.logical_and(at_row >= c * CHUNK, at_row <= place_col + c * CHUNK)
            take = jnp.where(jnp.logical_and(used, within), 1.0, 0.0).astype(BF16)
            out.append(sums[c] + mm(recvd[src], take))
        return tuple(out)

    sums = lax.fori_loop(
        0, MEMBERS, add_logs, tuple(jnp.zeros((H, CHUNK), F32) for c in range(CHUNKS))
    )
    total = jnp.zeros((H, HD), F32)
    for c in range(CHUNKS):
        rows = sums[c]
        rrow[c] = rows
        rcol[c] = jnp.concatenate([rows, jnp.zeros((HD - H, CHUNK), F32)], axis=0).T
        end = jnp.broadcast_to(rows[:, CHUNK - 1 : CHUNK], (H, HD))
        ends[c] = end
        total = total + end
    atot[...] = total
    for d in range(1, BACK + 1):

        @pl.when(tm + d < TM)
        def _():
            a_copy(d).start()

    load_w.wait()
    whole(recvx.at[half_every], xs.at[0], xr.at[0]).wait_recv()

    lane = lax.broadcasted_iota(jnp.int32, (CHUNK, HD), 1)

    def column(c, h):
        return jnp.sum(jnp.where(lane == h, rcol[c], 0.0), axis=1, keepdims=True)

    def project(j, carry):
        def columns(first):
            cols = pl.ds(pl.multiple_of(first, 256), 256)
            return mm(recvx[...], w[:, cols]).astype(BF16)

        kb[j] = columns(j * 256)
        vb[j] = columns(D + j * 256)
        for hh in range(2):
            h = 2 * j + hh
            lanes = slice(hh * HD, hh * HD + HD)
            local = None
            for c in range(CHUNKS):
                rows = slice(c * CHUNK, (c + 1) * CHUNK)
                end = ends[c, pl.ds(h, 1), :]
                fade = jnp.exp(end - column(c, h))
                keys = (kb[j, rows, lanes].astype(F32) * fade).astype(BF16)
                part = mm(keys, vb[j, rows, lanes], 0, 0)
                if c < CHUNKS - 1:
                    ub[c, h] = part
                local = part if c == 0 else jnp.exp(end) * local + part
            inc[h] = local
            ssend[0, h] = local.astype(BF16)
        return carry

    def gain(h, first, last):
        span = aprev[first, pl.ds(h, 1), :]
        for d in range(first + 1, last):
            span = span + aprev[d, pl.ds(h, 1), :]
        return span

    def round0(h, carry):
        got = srecv[0, h].astype(F32)
        exc[h] = got
        new = jnp.exp(atot[pl.ds(h, 1), :]) * got + inc[h]
        inc[h] = new
        ssend[1, h] = new.astype(BF16)
        return carry

    def round1(h, carry):
        got = srecv[1, h].astype(F32)
        before = gain(h, 0, 1)
        exc[h] = jnp.exp(before) * got + exc[h]
        new = jnp.exp(before + atot[pl.ds(h, 1), :]) * got + inc[h]
        ssend[2, h] = new.astype(BF16)
        return carry

    def round2(h, carry):
        got = srecv[2, h].astype(F32)
        exc[h] = jnp.exp(gain(h, 0, 3)) * got + exc[h]
        return carry

    def send_state(r, g):
        @pl.when(tm + (1 << r) < TM)
        def _():
            s_copy(r, g).start()

    def take_state(r, g):
        @pl.when(tm >= (1 << r))
        def _():
            s_copy(r, g).wait_recv()

    def emit(g):
        for p in range(2):
            q_copy(2 * g + p, 0, slice(0, CAP), half_every, to[0]).wait_recv()

        def head(hh, inner):
            h = g * GH + hh
            j = lax.div(h, 2)
            klanes = pl.ds(pl.multiple_of(lax.rem(h, 2) * HD, HD), HD)
            qlanes = pl.ds(pl.multiple_of(hh * HD, HD), HD)
            state = exc[h]
            for c in range(CHUNKS):
                rows = slice(c * CHUNK, (c + 1) * CHUNK)
                q = recvq[j, rows, klanes]
                k = kb[j, rows, klanes]
                v = vb[j, rows, klanes]
                col = column(c, h)
                spread = jnp.exp(jnp.minimum(col - rrow[c, pl.ds(h, 1), :], 0.0))
                scores = jnp.where(tri_r >= tri_c, mm(q, k, 1, 1) * spread, 0.0)
                s_hi, s_lo = split(scores)
                t_hi, t_lo = split(state)
                o = mm(s_hi, v) + mm(s_lo, v) + (mm(q, t_hi) + mm(q, t_lo)) * jnp.exp(col)
                scale = lax.rsqrt(jnp.mean(o * o, axis=1, keepdims=True) + 1e-06)
                osend[g, rows, qlanes] = (o * scale).astype(BF16)
                if c < CHUNKS - 1:
                    state = jnp.exp(ends[c, pl.ds(h, 1), :]) * state + ub[c, h]
            return inner

        lax.fori_loop(0, GH, head, 0)
        for i in reversed(range(PEERS)):
            o_copy(g, i, block(to[i]), mine).start()
        ret[g, mine, :] = osend[g, mine, :]

    def stage(s, carry):
        def turn(r, step):
            g = s - 1 - r

            @pl.when(jnp.logical_and(g >= 0, g < GROUPS))
            def _():
                take_state(r, g)
                lax.fori_loop(g * GH, (g + 1) * GH, step, 0)
                if r < 2:
                    send_state(r + 1, g)
                else:
                    emit(g)

        turn(2, round2)

        @pl.when(s < GROUPS)
        def _():
            lax.fori_loop(s * GP, (s + 1) * GP, project, 0)
            send_state(0, s)

        @pl.when(s == 0)
        def _():
            for d in range(1, BACK + 1):

                @pl.when(tm >= d)
                def _():
                    a_copy(d).wait_recv()

        turn(1, round1)
        turn(0, round0)
        return carry

    lax.fori_loop(0, GROUPS + 3, stage, 0)


    def out_copy(g):
        cols = pl.ds(pl.multiple_of(g * GW, GW), GW)
        return pltpu.make_async_copy(outb.at[:, cols], out_hbm.at[:, cols], out_sem.at[g])

    def finish(g, carry):
        o_copy(g, 0, every, every).wait_recv()
        for half in range(GW // 256):
            cols = slice(half * 256, half * 256 + 256)
            where = pl.ds(pl.multiple_of(g * GW + half * 256, 256), 256)
            got = ret[g, :, cols]
            outb[:, where] = (mm(chi[...], got) + mm(clo[...], got)).astype(BF16)
        out_copy(g).start()
        return carry

    lax.fori_loop(0, GROUPS, finish, 0)

    whole(slotp, sps.at[0], spr.at[0]).wait_send()
    whole(xp, xps.at[0], xpr.at[0]).wait_send()
    whole(qp, qps.at[0], qpr.at[0]).wait_send()
    whole(recvd.at[0:PEERS], ds_.at[0], dr.at[0]).wait_send()
    whole(recvx.at[half_every], xs.at[0], xr.at[0]).wait_send()
    whole(recvq.at[0:HALF_PEERS], qs.at[0], qr.at[0]).wait_send()
    whole(recvx.at[every], os_.at[0], or_.at[0]).wait_send()
    for g in range(GROUPS):
        out_copy(g).wait()
    for r in range(3):

        @pl.when(tm + (1 << r) < TM)
        def _():
            whole(ssend.at[r], ss.at[r], sr.at[r, 0]).wait_send()

    for d in range(1, BACK + 1):

        @pl.when(tm + d < TM)
        def _():
            a_copy(d).wait_send()


def on_device(tokens, queries, log_decay, route_ids, gate_weights, kv_weight):
    anywhere = pl.BlockSpec(memory_space=pl.ANY)
    near = pl.BlockSpec(memory_space=pltpu.VMEM)
    dma = pltpu.SemaphoreType.DMA
    return pl.pallas_call(
        kernel,
        out_shape=jax.ShapeDtypeStruct((TOK, D), BF16),
        in_specs=[anywhere, anywhere, near, near, near, anywhere],
        out_specs=anywhere,
        scratch_shapes=[
            pltpu.VMEM((TOK, D), BF16),
            pltpu.VMEM((TOK, D), BF16),
            pltpu.VMEM((D, 2 * D), BF16),
            pltpu.VMEM((ROWS + 128, TOK), BF16),
            pltpu.VMEM((QUARTERS, 2, HALF * CAP, TOK), BF16),
            pltpu.VMEM((TOK, ROWS), BF16),
            pltpu.VMEM((TOK, ROWS), BF16),
            pltpu.VMEM((8, TOK), F32),
            pltpu.VMEM((QUARTERS, 8, TOK), F32),
            pltpu.VMEM((QUARTERS, TOK, QW), BF16),
            pltpu.VMEM((QUARTERS, 2, TOK, 256), BF16),
            pltpu.VMEM((MEMBERS, H, 128), BF16),
            pltpu.VMEM((MEMBERS, H, 128), BF16),
            pltpu.VMEM((QUARTERS, 2, HALF * CAP, QW), BF16),
            pltpu.VMEM((ROWS, D), BF16),
            pltpu.VMEM((PAIRS, 2, HALF * CAP, 256), BF16),
            pltpu.VMEM((PAIRS, ROWS, 256), BF16),
            pltpu.VMEM((PAIRS, ROWS, 256), BF16),
            pltpu.VMEM((PAIRS, ROWS, 256), BF16),
            pltpu.VMEM((GROUPS, ROWS, GW), BF16),
            pltpu.VMEM((GROUPS, ROWS, GW), BF16),
            pltpu.VMEM((TOK, D), BF16),
            pltpu.VMEM((CHUNKS, CHUNK, HD), F32),
            pltpu.VMEM((CHUNKS, H, CHUNK), F32),
            pltpu.VMEM((CHUNKS, H, HD), F32),
            pltpu.VMEM((H, HD), F32),
            pltpu.VMEM((BACK, H, HD), F32),
            pltpu.VMEM((CHUNKS - 1, H, HD, HD), F32),
            pltpu.VMEM((H, HD, HD), F32),
            pltpu.VMEM((H, HD, HD), F32),
            pltpu.VMEM((3, H, HD, HD), BF16),
            pltpu.VMEM((3, H, HD, HD), BF16),
            dma((3,)),
            dma((1,)),
            dma((QUARTERS,)),
            dma((1,)),
            dma((QUARTERS,)),
            dma((1,)),
            dma((QUARTERS,)),
            dma((1,)),
            dma((1,)),
            dma((1,)),
            dma((1,)),
            dma((1,)),
            dma((PAIRS,)),
            dma((1,)),
            dma((GROUPS,)),
            dma((BACK,)),
            dma((BACK,)),
            dma((3,)),
            dma((3, GROUPS)),
            dma((GROUPS,)),
        ],
        compiler_params=pltpu.CompilerParams(
            collective_id=0, has_side_effects=True, vmem_limit_bytes=60 * 2**20
        ),
        name="memories",
    )(tokens, queries, log_decay.T, route_ids.T, gate_weights.T, kv_weight)


def solution(mesh):
    rows = P(("tm", "mem"), None)
    return jax.shard_map(
        on_device,
        mesh=mesh,
        in_specs=(rows, rows, rows, rows, rows, P("mem", None, None)),
        out_specs=rows,
        check_vma=False,
    )
```
